256 devices in a mesh: row: 16 (over z, y_hi), col: 16 (over y_lo, x, core).
Axes of the slice: x: 4, y: 4 (y_hi: 2, y_lo: 2; y = y_hi * 2 + y_lo), z: 8, core: 2. Of those that a mesh axis runs over, the one named last changes fastest.
Arguments:
- coarse_kernel: bfloat16 [1024, 1024], P('row', 'col'), may hold values from -0.031488349 to 0.031488349, as said below
- correlations: bfloat16 [256, 128, 128], P(('row', 'col')), may hold values from -0.5 to 0.5
- neighbor: int32 [256], P(('row', 'col')), may hold values from 0 to 7
- pair_weight: float32 [256, 256], P('row'), may hold values from 0.13 to 7.4, as said below
- energies: float32 [32768], P(('row', 'col')), may hold values from 0.5 to 2
- start_block: float32 [32768, 64], P(('row', 'col')), may hold values from -120 to 120
Outputs:
- residual: float32 [32768, 64], P(('row', 'col'))
- coefficients: float32 [3, 64, 64], replicated
The draws below stay inside these ranges and needn't reach their ends.
Inputs may be any that keep to these rules, and one draw needn't show every extreme that they name: coarse_kernel equals its transpose. pair_weight equals its transpose.
All inputs are finite; a program needn't handle non-finite values.
Results may differ from the reference program's by a relative error of at most 0.0085.
Values may be sent and summed in bfloat16 or wider, within the bound.
A program may use at most 64 MiB of HBM per device.

```python
import math
import jax
import jax.numpy as jnp
from jax import lax

B = 128
M = 64
NC = 8
NK = 256


def draw_coarse_kernel(key, part):
    noise_key = jax.random.fold_in(key, 11)
    noise = jnp.clip(jax.random.normal(noise_key, (NC * B, NC * B), jnp.float32), -4.0, 4.0)
    return ((noise + noise.T) * (0.7071 / math.sqrt(NK * B))).astype(jnp.bfloat16)


def draw_pair_weight(key, part):
    noise_key = jax.random.fold_in(key, 23)
    noise = jnp.clip(jax.random.normal(noise_key, (NK, NK), jnp.float32), -4.0, 4.0)
    return jnp.exp(0.25 * (noise + noise.T)).astype(jnp.float32)


def draw_start_block(key, part):
    total = NK * B
    position = jnp.arange(total, dtype=jnp.float32) / float(total - 1)
    row_scale = jnp.exp(position * math.log(30.0))
    noise_key = jax.random.fold_in(key, 37)
    values = jnp.clip(jax.random.normal(noise_key, (total, M), jnp.float32), -4.0, 4.0)
    return (values * row_scale[:, None]).astype(jnp.float32)


def with_ends(drawn, stream_key, low, top_value):
    spot = [jax.random.randint(jax.random.fold_in(stream_key, axis), (), 0, length) for axis, length in enumerate(drawn.shape)]
    main_axis = drawn.shape.index(max(drawn.shape))
    neighbour = spot[:main_axis] + [(spot[main_axis] + 1) % drawn.shape[main_axis]] + spot[main_axis + 1:]
    return drawn.at[tuple(spot)].set(low).at[tuple(neighbour)].set(top_value)


def block_scale(own_key, extent, pieces, least, top_value):
    factor_of, own = 1.0, jax.random.fold_in(own_key, 6)
    for axis_at, parts in pieces:
        draws = jnp.exp(jax.random.uniform(jax.random.fold_in(own, axis_at), (parts,), jnp.float32, least / len(pieces), top_value / len(pieces)))
        factor_of = factor_of * jnp.repeat(draws, extent[axis_at] // parts).reshape([-1 if axis == axis_at else 1 for axis in range(len(extent))])
    return factor_of


def normal_values(stream_key, extent, deviation, limit, pieces=(), kind=jnp.bfloat16):
    level = block_scale(stream_key, extent, pieces, -0.22, 0.18) if pieces else 1.0
    entries = jax.random.normal(stream_key, extent, jnp.float32) * deviation * level
    return jnp.minimum(jnp.maximum(entries, -limit), limit).astype(kind)


def setup_inputs(seed: int = 0) -> dict:
    keys = jax.random.split(jax.random.key(seed), 7)
    return {
        "coarse_kernel": draw_coarse_kernel(jax.random.fold_in(keys[6], 71), 0),
        "correlations": normal_values(keys[1], (NK, B, B), B ** -0.5, 0.5, ((0, 256),)),
        "neighbor": with_ends(jax.random.randint(keys[2], (NK,), 0, NC), jax.random.fold_in(keys[2], 1), 0, NC - 1).astype(jnp.int32),
        "pair_weight": draw_pair_weight(jax.random.fold_in(keys[6], 71), 0),
        "energies": jnp.clip(jnp.exp(math.log(2.0) - 1.3862944 * jax.random.uniform(keys[4], (NK * B,), jnp.float32) ** block_scale(keys[4], (NK * B,), ((0, 256),), -0.2, 0.2)), 0.5, 2.0),
        "start_block": draw_start_block(jax.random.fold_in(keys[6], 71), 0),
    }


highest = lax.Precision.HIGHEST

def coarse_products(coarse_kernel, correlations, neighbor):
    blocks = coarse_kernel.reshape(NC, B, NC, B)[:, :, neighbor, :].astype(jnp.float32)
    mapped = jnp.einsum('cakb,kbe->cake', blocks, correlations.astype(jnp.float32), precision=highest)
    return mapped.astype(jnp.bfloat16)

def apply_kernel(mapped, correlations, neighbor, pair_weight, vectors):
    group_size = 16 if NK % 16 == 0 else NK

    def one_group(index):
        offset = index * group_size
        row_correlation = lax.dynamic_slice_in_dim(correlations, offset, group_size, 0).astype(jnp.float32)
        row_neighbor = lax.dynamic_slice_in_dim(neighbor, offset, group_size, 0)
        weights = lax.dynamic_slice_in_dim(pair_weight, offset, group_size, 0)
        chosen = mapped[row_neighbor].astype(jnp.float32)
        product = jnp.einsum('kai,kaje->kije', row_correlation, chosen, precision=highest)
        kernel_rows = (product * weights[:, None, :, None]).astype(jnp.bfloat16)
        kernel_rows = kernel_rows.reshape(group_size * B, NK * B)
        return jnp.dot(kernel_rows.astype(jnp.float32), vectors.astype(jnp.float32), preferred_element_type=jnp.float32)
    result = lax.map(one_group, jnp.arange(NK // group_size, dtype=jnp.int32))
    return result.reshape(NK * B, M)

def gram_root(block):
    count = block.shape[0]
    gram_value = jnp.dot(block.T, block, precision=highest) / count
    lower = jnp.linalg.cholesky(gram_value)
    solved = jax.scipy.linalg.solve_triangular(lower, block.T, lower=True).T
    return (lower, solved)

def reference(coarse_kernel, correlations, neighbor, pair_weight, energies, start_block):
    count = NK * B
    mapped = coarse_products(coarse_kernel, correlations, neighbor)
    lower_first, basis = gram_root(start_block)
    image = energies[:, None] * basis + apply_kernel(mapped, correlations, neighbor, pair_weight, basis.astype(jnp.bfloat16))
    alpha_first = jnp.dot(basis.T, image, precision=highest) / count
    remainder = image - jnp.dot(basis, alpha_first, precision=highest)
    lower_next, second = gram_root(remainder)
    image_next = energies[:, None] * second + apply_kernel(mapped, correlations, neighbor, pair_weight, second.astype(jnp.bfloat16))
    image_next = image_next - jnp.dot(basis, lower_next, precision=highest)
    alpha_next = jnp.dot(second.T, image_next, precision=highest) / count
    residual = image_next - jnp.dot(second, alpha_next, precision=highest)
    return (residual, jnp.stack([alpha_first, lower_next, alpha_next]))
```

```python
import functools

import jax
import jax.numpy as jnp
from jax import lax
from jax.experimental import pallas as pl
from jax.experimental.pallas import tpu as pltpu
from jax.sharding import PartitionSpec as P

MESH = pl.DeviceIdType.MESH
HIGH = lax.Precision.HIGHEST
F32 = jnp.float32
BF16 = jnp.bfloat16
B = 128
M = 64
NX, NY, NZ = 4, 4, 8
NXY = NX * NY
TOTAL = 32768.0


def nn(a, b, precision=HIGH):
    return lax.dot_general(
        a, b, (((1,), (0,)), ((), ())), precision=precision, preferred_element_type=F32
    )


def nt(a, b, precision=HIGH):
    return lax.dot_general(
        a, b, (((1,), (1,)), ((), ())), precision=precision, preferred_element_type=F32
    )


def lanes(shape):
    return lax.broadcasted_iota(jnp.int32, shape, 1)


def rows(shape):
    return lax.broadcasted_iota(jnp.int32, shape, 0)


def packed_product(left, right):
    twice = jnp.concatenate([right, right], axis=0)
    upper = nt(left[: M // 2], twice)
    lower = nt(left[M // 2 :], twice)
    return jnp.where(lanes(upper.shape) < M, upper, lower)


def unpacked(packed):
    return jnp.concatenate([packed, pltpu.roll(packed, M, axis=1)], axis=0)


def factor(gram, out_ref):
    shape = (M, 2 * M)
    start = jnp.where(
        lanes(shape) < M, gram, jnp.where(lanes(shape) - M == rows(shape), 1.0, 0.0)
    )

    def eight(block, matrix):
        done = []
        for s in range(8):
            root = lax.rsqrt(matrix[s : s + 1, s : s + 1])
            row = matrix[s : s + 1, :] * root
            column = matrix[:, s : s + 1] * root
            done.append(row)
            matrix = matrix - column * row
        finished = pltpu.roll(jnp.concatenate(done, axis=0), 8 * block, axis=1)
        out_ref[pl.ds(pl.multiple_of(8 * block, 8), 8), :] = finished
        matrix = jnp.concatenate([matrix[8:], matrix[:8]], axis=0)
        return pltpu.roll(matrix, 2 * M - 8, axis=1)

    lax.fori_loop(0, M // 8, eight, start)
    result = out_ref[...]
    upper = jnp.where(lanes(shape) >= rows(shape), result, 0.0)[:, :M]
    inverse = pltpu.roll(result, M, axis=1)[:, :M]
    return upper, inverse


def kernel(
    coarse_ref, corr_ref, near_ref, weight_ref, energy_ref, start_ref,
    residual_ref, coef_ref,
    cbuf, chalf, near_k, near_own, near_xy, near_z, near_xy_s, near_z_s, w_other, w_s,
    gk, gxy, gz, gsend, fac,
    ubuf, tbuf, ypart, ysend, yk, rsend, rbuf,
    ak, asend, az, axy, afull, hk, hxy, hz, hsend,
    send, recv, local,
):
    row, col = lax.axis_index("row"), lax.axis_index("col")
    z, yh = row // 2, row % 2
    yl, x, k = col // 8, (col // 2) % 4, col % 2
    y = yh * 2 + yl
    me_xy = y * NX + x

    def device(x_, y_, z_, k_):
        return (z_ * 2 + y_ // 2, (y_ % 2) * 8 + x_ * 2 + k_)

    sibling = device(x, y, z, 1 - k)
    x_ring = [device((x + d) % NX, y, z, k) for d in range(1, NX)]
    y_ring = [device(x, (y + d) % NY, z, k) for d in range(1, NY)]
    z_ring = [device(x, y, (z + d) % NZ, k) for d in range(1, NZ)]
    plane = [
        device((x + dx) % NX, (y + dy) % NY, z, k)
        for dy in range(NY)
        for dx in range(NX)
        if dx or dy
    ]
    count = [0]
    sent = []

    def push(src, dst, targets, like=None):
        i = count[0]
        count[0] += 1
        for target in targets:
            pltpu.make_async_remote_copy(
                src_ref=src, dst_ref=dst, send_sem=send.at[i], recv_sem=recv.at[i],
                device_id=target, device_id_type=MESH,
            ).start()
        like = dst if like is None else like
        sent.append((i, like))

        def wait():
            pltpu.make_async_copy(like, like, recv.at[i]).wait()

        return wait

    barrier = pltpu.get_barrier_semaphore()
    partners = [sibling] + plane + z_ring
    for target in partners:
        pl.semaphore_signal(barrier, inc=1, device_id=target, device_id_type=MESH)
    near_own[...] = jnp.full((8, B), near_ref[0], jnp.int32)
    start_t = start_ref[...].T
    gk[0] = packed_product(start_t, start_t)
    pl.semaphore_wait(barrier, len(partners))

    other_half = pl.ds(pl.multiple_of((1 - k) * 32, 32), 32)
    own_half = pl.ds(pl.multiple_of(k * 32, 32), 32)
    got_half = push(coarse_ref.at[other_half], chalf, [sibling])
    got_gk = push(gk.at[0], gk.at[1], [sibling])
    got_near_k = push(near_own, near_k, [sibling])

    got_half()
    shape = (M, B)
    place_own = jnp.where(lanes(shape) == rows(shape) + M * k, 1.0, 0.0).astype(BF16)
    place_sib = jnp.where(lanes(shape) == rows(shape) + M * (1 - k), 1.0, 0.0).astype(BF16)
    strip = nn(coarse_ref[own_half, :], place_own, None) + nn(chalf[...], place_sib, None)
    cbuf[z, yl, x, yh, k] = strip.astype(BF16)
    mine = cbuf.at[z, yl, x, yh, k]
    got_a = push(mine, mine, z_ring, cbuf.at[pl.ds(0, 7), 0, 0, 0, 0])

    got_gk()
    gxy[me_xy] = gk[0] + gk[1]
    got_gxy = push(gxy.at[me_xy], gxy.at[me_xy], plane, gxy.at[pl.ds(0, NXY - 1)])
    got_w = push(weight_ref, w_other, [y_ring[1]])
    near_xy[me_xy] = near_own[...]
    got_near_xy = push(near_xy.at[me_xy], near_xy.at[me_xy], plane, near_xy.at[pl.ds(0, NXY - 1)])
    got_near_k()
    near_z[z] = jnp.where(rows((8, B)) == 0, near_own[...], near_k[...])
    got_near_z = push(near_z.at[z], near_z.at[z], z_ring, near_z.at[pl.ds(0, NZ - 1)])

    got_a()
    b_first = cbuf.at[pl.ds(0, 4), yl, x, yh, k]
    b_second = cbuf.at[pl.ds(4, 4), yl, x, yh, k]
    twelve = cbuf.at[pl.ds(0, 6), :, 0, 0, 0]
    got_b1 = push(b_first, b_first, x_ring, twelve)
    got_b2 = push(b_second, b_second, y_ring, twelve)

    got_gxy()
    gz[z] = jnp.sum(gxy[...], axis=0)
    got_gz = push(gz.at[z], gz.at[z], z_ring, gz.at[pl.ds(0, NZ - 1)])

    got_b1()
    c_first = cbuf.at[pl.ds(0, 4), yl, :, yh, k]
    c_second = cbuf.at[pl.ds(4, 4), :, x, :, k]
    fortyeight = cbuf.at[pl.ds(0, 6), :, :, 0, 0]
    got_c1 = push(c_first, c_first, y_ring, fortyeight)
    got_b2()
    got_c2 = push(c_second, c_second, x_ring, fortyeight)

    got_w()
    got_near_xy()
    got_near_z()
    locals_ = [
        pltpu.make_async_copy(weight_ref, w_s.at[yh], local.at[0]),
        pltpu.make_async_copy(w_other, w_s.at[1 - yh], local.at[1]),
        pltpu.make_async_copy(near_xy, near_xy_s, local.at[2]),
        pltpu.make_async_copy(near_z, near_z_s, local.at[3]),
    ]
    for c in locals_:
        c.start()

    corr = corr_ref[0].astype(F32)

    got_gz()
    gram = unpacked(jnp.sum(gz[...], axis=0) * (1.0 / TOTAL))
    _, inverse0 = factor(gram, fac.at[0])
    basis = nn(inverse0, start_t)

    def gather(step, vectors):
        ubuf[step, me_xy] = nt(vectors, corr).astype(BF16)
        mine_ = ubuf.at[step, me_xy]
        return push(mine_, mine_, plane, ubuf.at[step, pl.ds(0, NXY - 1)])

    got_u = gather(0, basis)
    for c in locals_:
        c.wait()
    got_c1()
    got_c2()
    half_all = cbuf.at[:, :, :, :, k]
    got_d = push(half_all, half_all, [sibling])
    got_d()
    got_u()

    def apply(step):
        def one_source(q, _):
            block = cbuf[near_xy_s[q, 0, 0]].reshape(8, B, B)
            vector = ubuf[step, q]
            for c in range(8):
                tbuf[q, c] = nn(vector, block[c], None)
            return 0

        lax.fori_loop(0, NXY, one_source, 0)

        def target(z_, other, out):
            near = near_z_s[z_, other, 0]
            kk = jnp.where(other == 1, 1 - k, k) if not isinstance(other, int) else (1 - k if other else k)
            place = z_ * 32 + yh * 16 + yl * 8 + x * 2 + kk
            total = jnp.zeros((M, B), F32)
            for q in range(NXY):
                qy, qx = q // NX, q % NX
                w = w_s[qy // 2, (qy % 2) * 8 + qx * 2 + k, place]
                total = total + w * tbuf[q, near]
            out[z_] = total

        def for_sibling(z_, _):
            target(z_, 1, ysend.at[step])
            return 0

        def for_own(z_, _):
            target(z_, 0, ypart)
            return 0

        lax.fori_loop(0, NZ, for_sibling, 0)
        got_yk = push(ysend.at[step], yk.at[step], [sibling])
        lax.fori_loop(0, NZ, for_own, 0)
        got_yk()
        total = ypart[...] + yk[step]
        rsend[step] = total.astype(BF16)
        i = count[0]
        count[0] += 1
        for d in range(1, NZ):
            there = (z + d) % NZ
            pltpu.make_async_remote_copy(
                src_ref=rsend.at[step, there], dst_ref=rbuf.at[step, z],
                send_sem=send.at[i], recv_sem=recv.at[i],
                device_id=z_ring[d - 1], device_id_type=MESH,
            ).start()
        like = rbuf.at[step, pl.ds(0, NZ - 1)]
        sent.append((i, like))
        rbuf[step, z] = jnp.zeros((M, B), BF16)
        own = ypart[z] + yk[step, z]

        def result():
            pltpu.make_async_copy(like, like, recv.at[i]).wait()
            summed = own + jnp.sum(rbuf[step].astype(F32), axis=0)
            return nn(summed, corr)

        return result

    energy = energy_ref[...]
    image = energy * basis + apply(0)()

    got_u = gather(1, image)
    ak[0] = nt(image, jnp.concatenate([basis, image], axis=0))
    got_ak = push(ak.at[0], ak.at[1], [sibling])
    got_ak()
    asend[...] = (ak[0] + ak[1]).reshape(NZ, 8, B)
    az[z] = asend[z]
    i_az = count[0]
    count[0] += 1
    for d in range(1, NZ):
        there = (z + d) % NZ
        pltpu.make_async_remote_copy(
            src_ref=asend.at[there], dst_ref=az.at[z], send_sem=send.at[i_az], recv_sem=recv.at[i_az],
            device_id=z_ring[d - 1], device_id_type=MESH,
        ).start()
    like_az = az.at[pl.ds(0, NZ - 1)]
    sent.append((i_az, like_az))

    got_u()
    second_sum = apply_started = None
    pltpu.make_async_copy(like_az, like_az, recv.at[i_az]).wait()
    axy[me_xy] = jnp.sum(az[...], axis=0)
    got_axy = push(axy.at[me_xy], axy.at[me_xy], plane, axy.at[pl.ds(0, NXY - 1)])
    second_sum = apply(1)
    got_axy()
    afull[z] = jnp.sum(axy[...], axis=0)
    got_afull = push(afull.at[z], afull.at[z], z_ring, afull.at[pl.ds(0, NZ - 1)])
    got_afull()
    both = afull[...].reshape(M, B) * (1.0 / TOTAL)
    alpha_t = both[:, :M]
    next_gram = pltpu.roll(both, M, axis=1)[:, :M] - nt(alpha_t, alpha_t)
    next_gram = jnp.concatenate([next_gram, next_gram], axis=1)
    upper1, inverse1 = factor(next_gram, fac.at[1])
    second = nn(inverse1, image - nn(alpha_t, basis))
    minus = nn(upper1, basis)
    less = energy * image - nn(alpha_t, image)
    image_next = nn(inverse1, less + second_sum()) - minus

    hsend[...] = packed_product(image_next, second)
    got_hk = push(hsend, hk, [sibling])
    got_hk()
    hxy[me_xy] = hsend[...] + hk[...]
    got_hxy = push(hxy.at[me_xy], hxy.at[me_xy], plane, hxy.at[pl.ds(0, NXY - 1)])
    got_hxy()
    hz[z] = jnp.sum(hxy[...], axis=0)
    got_hz = push(hz.at[z], hz.at[z], z_ring, hz.at[pl.ds(0, NZ - 1)])
    coef_ref[0] = alpha_t
    coef_ref[1] = upper1
    got_hz()
    alpha_next_t = unpacked(jnp.sum(hz[...], axis=0) * (1.0 / TOTAL))[:, :M]
    coef_ref[2] = alpha_next_t
    residual_ref[...] = image_next - nn(alpha_next_t, second)

    for i, like in sent:
        pltpu.make_async_copy(like, like, send.at[i]).wait()


def on_device(coarse_kernel, correlations, neighbor, pair_weight, energies, start_block):
    vmem = pl.BlockSpec(memory_space=pltpu.VMEM)
    smem = pl.BlockSpec(memory_space=pltpu.SMEM)
    residual_t, coefficients_t = pl.pallas_call(
        kernel,
        out_shape=(
            jax.ShapeDtypeStruct((M, B), F32),
            jax.ShapeDtypeStruct((3, M, M), F32),
        ),
        in_specs=[vmem, vmem, smem, vmem, vmem, vmem],
        out_specs=(vmem, vmem),
        scratch_shapes=[
            pltpu.VMEM((8, 2, 4, 2, 2, 32, B), BF16),
            pltpu.VMEM((32, M), BF16),
            pltpu.VMEM((8, B), jnp.int32),
            pltpu.VMEM((8, B), jnp.int32),
            pltpu.VMEM((NXY, 8, B), jnp.int32),
            pltpu.VMEM((NZ, 8, B), jnp.int32),
            pltpu.SMEM((NXY, 8, B), jnp.int32),
            pltpu.SMEM((NZ, 8, B), jnp.int32),
            pltpu.VMEM((16, 256), F32),
            pltpu.SMEM((2, 16, 256), F32),
            pltpu.VMEM((2, M // 2, B), F32),
            pltpu.VMEM((NXY, M // 2, B), F32),
            pltpu.VMEM((NZ, M // 2, B), F32),
            pltpu.VMEM((M // 2, B), F32),
            pltpu.VMEM((2, M, B), F32),
            pltpu.VMEM((2, NXY, M, B), BF16),
            pltpu.VMEM((NXY, 8, M, B), F32),
            pltpu.VMEM((NZ, M, B), F32),
            pltpu.VMEM((2, NZ, M, B), F32),
            pltpu.VMEM((2, NZ, M, B), F32),
            pltpu.VMEM((2, NZ, M, B), BF16),
            pltpu.VMEM((2, NZ, M, B), BF16),
            pltpu.VMEM((2, M, B), F32),
            pltpu.VMEM((NZ, 8, B), F32),
            pltpu.VMEM((NZ, 8, B), F32),
            pltpu.VMEM((NXY, 8, B), F32),
            pltpu.VMEM((NZ, 8, B), F32),
            pltpu.VMEM((M // 2, B), F32),
            pltpu.VMEM((NXY, M // 2, B), F32),
            pltpu.VMEM((NZ, M // 2, B), F32),
            pltpu.VMEM((M // 2, B), F32),
            pltpu.SemaphoreType.DMA((32,)),
            pltpu.SemaphoreType.DMA((32,)),
            pltpu.SemaphoreType.DMA((4,)),
        ],
        compiler_params=pltpu.CompilerParams(
            collective_id=0, has_side_effects=True, vmem_limit_bytes=40 << 20
        ),
    )(coarse_kernel, correlations, neighbor, pair_weight, energies.reshape(1, B), start_block)
    return residual_t.T, jnp.swapaxes(coefficients_t, 1, 2)


def solution(mesh):
    both = ("row", "col")
    return jax.shard_map(
        on_device,
        mesh=mesh,
        in_specs=(
            P("row", "col"),
            P(both, None, None),
            P(both),
            P("row", None),
            P(both),
            P(both, None),
        ),
        out_specs=(P(both, None), P()),
        check_vma=False,
    )
```

```python
import functools

import jax
import jax.numpy as jnp
from jax import lax
from jax.experimental import pallas as pl
from jax.experimental.pallas import tpu as pltpu
from jax.sharding import PartitionSpec as P

MESH = pl.DeviceIdType.MESH
HIGH = lax.Precision.HIGHEST
F32 = jnp.float32
BF16 = jnp.bfloat16
B = 128
M = 64
NX, NY, NZ = 4, 4, 8
NXY = NX * NY
TOTAL = 32768.0


def nn(a, b, precision=HIGH):
    return lax.dot_general(
        a, b, (((1,), (0,)), ((), ())), precision=precision, preferred_element_type=F32
    )


def nt(a, b, precision=HIGH):
    return lax.dot_general(
        a, b, (((1,), (1,)), ((), ())), precision=precision, preferred_element_type=F32
    )


def lanes(shape):
    return lax.broadcasted_iota(jnp.int32, shape, 1)


def rows(shape):
    return lax.broadcasted_iota(jnp.int32, shape, 0)


def packed_product(left, right):
    twice = jnp.concatenate([right, right], axis=0)
    upper = nt(left[: M // 2], twice)
    lower = nt(left[M // 2 :], twice)
    return jnp.where(lanes(upper.shape) < M, upper, lower)


def unpacked(packed):
    return jnp.concatenate([packed, pltpu.roll(packed, M, axis=1)], axis=0)


def factor(gram, out_ref):
    shape = (M, 2 * M)
    start = jnp.where(
        lanes(shape) < M, gram, jnp.where(lanes(shape) - M == rows(shape), 1.0, 0.0)
    )

    def four(matrix, s):
        c = [jnp.broadcast_to(matrix[:, s + i : s + i + 1], shape) for i in range(4)]
        r = [matrix[s + i : s + i + 1, :] for i in range(4)]
        p = [[c[j][s + i : s + i + 1, :] for j in range(4)] for i in range(4)]

        def pair(i):
            first, cross, last = p[i][i], p[i][i + 1], p[i + 1][i + 1]
            det = first * last - cross * cross
            root = lax.rsqrt(det)
            inverse = root * root
            scale = lax.rsqrt(first)
            upper = r[i] * scale
            lower = (r[i + 1] - r[i] * (cross * scale * scale)) * (root * first * scale)
            return last * inverse, -cross * inverse, first * inverse, [upper, lower]

        i00, i01, i11, done = pair(0)
        for i in (2, 3):
            w0 = p[0][i] * i00 + p[1][i] * i01
            w1 = p[0][i] * i01 + p[1][i] * i11
            r[i] = r[i] - w0 * r[0] - w1 * r[1]
            c[i] = c[i] - w0 * c[0] - w1 * c[1]
            for j in range(i, 4):
                p[i][j] = p[i][j] - w0 * p[0][j] - w1 * p[1][j]
        j00, j01, j11, more = pair(2)
        matrix = matrix - (
            c[0] * (i00 * r[0] + i01 * r[1])
            + c[1] * (i01 * r[0] + i11 * r[1])
            + c[2] * (j00 * r[2] + j01 * r[3])
            + c[3] * (j01 * r[2] + j11 * r[3])
        )
        return matrix, done + more

    def eight(block, matrix):
        matrix, done = four(matrix, 0)
        matrix, more = four(matrix, 4)
        finished = pltpu.roll(jnp.concatenate(done + more, axis=0), 8 * block, axis=1)
        out_ref[pl.ds(pl.multiple_of(8 * block, 8), 8), :] = finished
        matrix = jnp.concatenate([matrix[8:], matrix[:8]], axis=0)
        return pltpu.roll(matrix, 2 * M - 8, axis=1)

    lax.fori_loop(0, M // 8, eight, start)
    result = out_ref[...]
    upper = jnp.where(lanes(shape) >= rows(shape), result, 0.0)[:, :M]
    inverse = pltpu.roll(result, M, axis=1)[:, :M]
    return upper, inverse


def kernel(
    coarse_ref, corr_ref, near_ref, weight_ref, energy_ref, start_ref,
    residual_ref, coef_ref,
    cbuf, chalf, near_k, near_own, near_xy, near_z, near_xy_s, near_z_s, w_other, w_s,
    gk, gxy, gz, gsend, fac,
    ubuf, tbuf, ypart, ysend, yk, rsend, rbuf,
    uz, ak, asend, az, axy, afull, hk, hxy, hz, hsend,
    send, recv, local,
):
    row, col = lax.axis_index("row"), lax.axis_index("col")
    z, yh = row // 2, row % 2
    yl, x, k = col // 8, (col // 2) % 4, col % 2
    y = yh * 2 + yl
    me_xy = y * NX + x

    def device(x_, y_, z_, k_):
        return (z_ * 2 + y_ // 2, (y_ % 2) * 8 + x_ * 2 + k_)

    sibling = device(x, y, z, 1 - k)
    x_ring = [device((x + d) % NX, y, z, k) for d in range(1, NX)]
    y_ring = [device(x, (y + d) % NY, z, k) for d in range(1, NY)]
    z_ring = [device(x, y, (z + d) % NZ, k) for d in range(1, NZ)]
    plane = [
        device((x + dx) % NX, (y + dy) % NY, z, k)
        for dy in range(NY)
        for dx in range(NX)
        if dx or dy
    ]
    count = [0]
    sent = []
    pending = []

    def push(src, dst, targets, like=None):
        i = count[0]
        count[0] += 1
        for d, target in enumerate(targets):
            pltpu.make_async_remote_copy(
                src_ref=src(d) if callable(src) else src, dst_ref=dst,
                send_sem=send.at[i], recv_sem=recv.at[i],
                device_id=target, device_id_type=MESH,
            ).start()
        like = dst if like is None else like
        sent.append((i, like))

        def wait():
            pltpu.make_async_copy(like, like, recv.at[i]).wait()
            pending.remove(wait)

        pending.append(wait)
        return wait

    barrier = pltpu.get_barrier_semaphore()
    partners = [sibling] + plane + z_ring
    for target in partners:
        pl.semaphore_signal(barrier, inc=1, device_id=target, device_id_type=MESH)
    near_own[...] = jnp.full((8, B), near_ref[0], jnp.int32)
    start_t = start_ref[...]
    gk[0] = packed_product(start_t, start_t)
    pl.semaphore_wait(barrier, len(partners))

    other_half = pl.ds(pl.multiple_of((1 - k) * 32, 32), 32)
    own_half = pl.ds(pl.multiple_of(k * 32, 32), 32)
    got_half = push(coarse_ref.at[other_half], chalf, [sibling])
    got_gk = push(gk.at[0], gk.at[1], [sibling])
    got_near_k = push(near_own, near_k, [sibling])

    got_half()
    shape = (M, B)
    place_own = jnp.where(lanes(shape) == rows(shape) + M * k, 1.0, 0.0).astype(BF16)
    place_sib = jnp.where(lanes(shape) == rows(shape) + M * (1 - k), 1.0, 0.0).astype(BF16)
    strip = nn(coarse_ref[own_half, :], place_own, None) + nn(chalf[...], place_sib, None)
    cbuf[z, yl, x, yh, k] = strip.astype(BF16)
    mine = cbuf.at[z, yl, x, yh, k]
    got_a = push(mine, mine, z_ring, cbuf.at[pl.ds(0, 7), 0, 0, 0, 0])

    got_gk()
    gxy[me_xy] = gk[0] + gk[1]
    got_gxy = push(gxy.at[me_xy], gxy.at[me_xy], plane, gxy.at[pl.ds(0, NXY - 1)])
    got_w = push(weight_ref, w_other, [y_ring[1]])
    near_xy[me_xy] = near_own[...]
    got_near_xy = push(near_xy.at[me_xy], near_xy.at[me_xy], plane, near_xy.at[pl.ds(0, NXY - 1)])
    got_near_k()
    near_z[z] = jnp.where(rows((8, B)) == 0, near_own[...], near_k[...])
    got_near_z = push(near_z.at[z], near_z.at[z], z_ring, near_z.at[pl.ds(0, NZ - 1)])

    got_a()
    b_first = cbuf.at[pl.ds(0, 4), yl, x, yh, k]
    b_second = cbuf.at[pl.ds(4, 4), yl, x, yh, k]
    twelve = cbuf.at[pl.ds(0, 6), :, 0, 0, 0]
    got_b1 = push(b_first, b_first, x_ring, twelve)
    got_b2 = push(b_second, b_second, y_ring, twelve)

    got_gxy()
    gz[z] = jnp.sum(gxy[...], axis=0)
    got_gz = push(gz.at[z], gz.at[z], z_ring, gz.at[pl.ds(0, NZ - 1)])

    got_b1()
    c_first = cbuf.at[pl.ds(0, 4), yl, :, yh, k]
    c_second = cbuf.at[pl.ds(4, 4), :, x, :, k]
    fortyeight = cbuf.at[pl.ds(0, 6), :, :, 0, 0]
    got_c1 = push(c_first, c_first, y_ring, fortyeight)
    got_b2()
    got_c2 = push(c_second, c_second, x_ring, fortyeight)

    got_w()
    got_near_xy()
    got_near_z()
    locals_ = [
        pltpu.make_async_copy(weight_ref, w_s.at[yh], local.at[0]),
        pltpu.make_async_copy(w_other, w_s.at[1 - yh], local.at[1]),
        pltpu.make_async_copy(near_xy, near_xy_s, local.at[2]),
        pltpu.make_async_copy(near_z, near_z_s, local.at[3]),
    ]
    for c in locals_:
        c.start()
        pending.append(c.wait)

    corr = corr_ref[0].astype(F32)

    got_gz()
    gram = unpacked(jnp.sum(gz[...], axis=0) * (1.0 / TOTAL))
    _, inverse0 = factor(gram, fac.at[0])
    basis = nn(inverse0, start_t)

    def gather(step, vectors):
        ubuf[step, me_xy] = nt(vectors, corr).astype(BF16)
        mine_ = ubuf.at[step, me_xy]
        return push(mine_, mine_, plane, ubuf.at[step, pl.ds(0, NXY - 1)])

    got_u = gather(0, basis)
    for c in locals_:
        c.wait()
        pending.remove(c.wait)
    got_c1()
    got_c2()
    half_all = cbuf.at[:, :, :, :, k]
    got_d = push(half_all, half_all, [sibling])
    got_d()
    got_u()

    def apply(step):
        def one_source(q, _):
            block = cbuf[near_xy_s[q, 0, 0]].reshape(8, B, B)
            vector = ubuf[step, q]
            for c in range(8):
                tbuf[q, c] = nn(vector, block[c], None)
            return 0

        lax.fori_loop(0, NXY, one_source, 0, unroll=4)

        def target(z_, other, out):
            near = near_z_s[z_, other, 0]
            place = z_ * 32 + yh * 16 + yl * 8 + x * 2 + (1 - k if other else k)
            total = jnp.zeros((M, B), F32)
            for q in range(NXY):
                qy, qx = q // NX, q % NX
                w = w_s[qy // 2, (qy % 2) * 8 + qx * 2 + k, place]
                total = total + w * tbuf[q, near]
            out[z_] = total

        def for_sibling(z_, _):
            target(z_, 1, ysend.at[step])
            return 0

        def for_own(z_, _):
            target(z_, 0, ypart)
            return 0

        lax.fori_loop(0, NZ, for_sibling, 0)
        got_yk = push(ysend.at[step], yk.at[step], [sibling])
        lax.fori_loop(0, NZ, for_own, 0)
        got_yk()
        total = ypart[...] + yk[step]
        rsend[step] = total.astype(BF16)
        got_r = push(
            lambda d: rsend.at[step, (z + d + 1) % NZ], rbuf.at[step, z], z_ring,
            rbuf.at[step, pl.ds(0, NZ - 1)],
        )
        rbuf[step, z] = jnp.zeros((M, B), BF16)
        own = ypart[z] + yk[step, z]

        def result():
            got_r()
            summed = own + jnp.sum(rbuf[step].astype(F32), axis=0)
            return nn(summed, corr)

        return result

    energy = energy_ref[...]
    image = energy * basis + apply(0)()

    got_u = gather(1, image)
    uz[z] = ubuf[1, me_xy]
    got_uz = push(uz.at[z], uz.at[z], z_ring, uz.at[pl.ds(0, NZ - 1)])
    ak[0] = nt(image, jnp.concatenate([basis, image], axis=0))
    got_ak = push(ak.at[0], ak.at[1], [sibling])
    energy_product = packed_product(image, energy * image)
    got_ak()
    asend[...] = (ak[0] + ak[1]).reshape(NZ, 8, B)
    az[z] = asend[z]
    got_az = push(
        lambda d: asend.at[(z + d + 1) % NZ], az.at[z], z_ring, az.at[pl.ds(0, NZ - 1)]
    )

    got_az()
    axy[me_xy] = jnp.sum(az[...], axis=0)
    got_axy = push(axy.at[me_xy], axy.at[me_xy], plane, axy.at[pl.ds(0, NXY - 1)])
    got_u()
    second_sum = apply(1)

    got_uz()
    upper = jnp.zeros((M // 2, B), F32)
    lower = upper
    for d in range(NZ):
        twice = jnp.concatenate([rsend[1, d], rsend[1, d]], axis=0)
        vector = uz[d]
        upper = upper + nt(vector[: M // 2], twice, None)
        lower = lower + nt(vector[M // 2 :], twice, None)
    hsend[...] = energy_product + jnp.where(lanes(upper.shape) < M, upper, lower)
    got_hk = push(hsend, hk, [sibling])
    got_axy()
    afull[z] = jnp.sum(axy[...], axis=0)
    got_afull = push(afull.at[z], afull.at[z], z_ring, afull.at[pl.ds(0, NZ - 1)])
    got_hk()
    hxy[me_xy] = hsend[...] + hk[...]
    got_hxy = push(hxy.at[me_xy], hxy.at[me_xy], plane, hxy.at[pl.ds(0, NXY - 1)])
    image_sum = energy * image + second_sum()
    got_hxy()
    hz[z] = jnp.sum(hxy[...], axis=0)
    got_hz = push(hz.at[z], hz.at[z], z_ring, hz.at[pl.ds(0, NZ - 1)])
    got_afull()
    both = afull[...].reshape(M, B) * (1.0 / TOTAL)
    alpha_t = both[:, :M]
    square = pltpu.roll(both, M, axis=1)[:, :M]
    next_gram = square - nt(alpha_t, alpha_t)
    upper1, inverse1 = factor(jnp.concatenate([next_gram, next_gram], axis=1), fac.at[1])
    second = nn(inverse1, image - nn(alpha_t, basis))
    image_next = nn(inverse1, image_sum - nn(alpha_t, image)) - nn(upper1, basis)
    known = (
        nt(alpha_t, nn(alpha_t, alpha_t)) - nn(alpha_t, square) - nt(square, alpha_t)
    )
    coef_ref[0] = alpha_t
    coef_ref[1] = upper1
    got_hz()
    middle = unpacked(jnp.sum(hz[...], axis=0) * (1.0 / TOTAL))[:, :M] + known
    alpha_next_t = nn(inverse1, nt(middle, inverse1))
    coef_ref[2] = alpha_next_t
    residual_ref[...] = image_next - nn(alpha_next_t, second)

    for i, like in sent:
        pltpu.make_async_copy(like, like, send.at[i]).wait()


def on_device(coarse_kernel, correlations, neighbor, pair_weight, energies, start_block):
    vmem = pl.BlockSpec(memory_space=pltpu.VMEM)
    smem = pl.BlockSpec(memory_space=pltpu.SMEM)
    residual_t, coefficients_t = pl.pallas_call(
        kernel,
        out_shape=(
            jax.ShapeDtypeStruct((M, B), F32),
            jax.ShapeDtypeStruct((3, M, M), F32),
        ),
        in_specs=[vmem, vmem, smem, vmem, vmem, vmem],
        out_specs=(vmem, vmem),
        scratch_shapes=[
            pltpu.VMEM((8, 2, 4, 2, 2, 32, B), BF16),
            pltpu.VMEM((32, M), BF16),
            pltpu.VMEM((8, B), jnp.int32),
            pltpu.VMEM((8, B), jnp.int32),
            pltpu.VMEM((NXY, 8, B), jnp.int32),
            pltpu.VMEM((NZ, 8, B), jnp.int32),
            pltpu.SMEM((NXY, 8, B), jnp.int32),
            pltpu.SMEM((NZ, 8, B), jnp.int32),
            pltpu.VMEM((16, 256), F32),
            pltpu.SMEM((2, 16, 256), F32),
            pltpu.VMEM((2, M // 2, B), F32),
            pltpu.VMEM((NXY, M // 2, B), F32),
            pltpu.VMEM((NZ, M // 2, B), F32),
            pltpu.VMEM((M // 2, B), F32),
            pltpu.VMEM((2, M, B), F32),
            pltpu.VMEM((2, NXY, M, B), BF16),
            pltpu.VMEM((NXY, 8, M, B), F32),
            pltpu.VMEM((NZ, M, B), F32),
            pltpu.VMEM((2, NZ, M, B), F32),
            pltpu.VMEM((2, NZ, M, B), F32),
            pltpu.VMEM((2, NZ, M, B), BF16),
            pltpu.VMEM((2, NZ, M, B), BF16),
            pltpu.VMEM((NZ, M, B), BF16),
            pltpu.VMEM((2, M, B), F32),
            pltpu.VMEM((NZ, 8, B), F32),
            pltpu.VMEM((NZ, 8, B), F32),
            pltpu.VMEM((NXY, 8, B), F32),
            pltpu.VMEM((NZ, 8, B), F32),
            pltpu.VMEM((M // 2, B), F32),
            pltpu.VMEM((NXY, M // 2, B), F32),
            pltpu.VMEM((NZ, M // 2, B), F32),
            pltpu.VMEM((M // 2, B), F32),
            pltpu.SemaphoreType.DMA((32,)),
            pltpu.SemaphoreType.DMA((32,)),
            pltpu.SemaphoreType.DMA((4,)),
        ],
        compiler_params=pltpu.CompilerParams(
            collective_id=0, has_side_effects=True, vmem_limit_bytes=40 << 20
        ),
    )(coarse_kernel, correlations, neighbor, pair_weight, energies.reshape(1, B), start_block.T)
    return residual_t.T, jnp.swapaxes(coefficients_t, 1, 2)


def solution(mesh):
    both = ("row", "col")
    return jax.shard_map(
        on_device,
        mesh=mesh,
        in_specs=(
            P("row", "col"),
            P(both, None, None),
            P(both),
            P("row", None),
            P(both),
            P(both, None),
        ),
        out_specs=(P(both, None), P()),
        check_vma=False,
    )
```

```python
import functools

import jax
import jax.numpy as jnp
from jax import lax
from jax.experimental import pallas as pl
from jax.experimental.pallas import tpu as pltpu
from jax.sharding import PartitionSpec as P

MESH = pl.DeviceIdType.MESH
HIGH = lax.Precision.HIGHEST
F32 = jnp.float32
BF16 = jnp.bfloat16
B = 128
M = 64
NX, NY, NZ = 4, 4, 8
NXY = NX * NY
TOTAL = 32768.0


def nn(a, b, precision=HIGH):
    return lax.dot_general(
        a, b, (((1,), (0,)), ((), ())), precision=precision, preferred_element_type=F32
    )


def nt(a, b, precision=HIGH):
    return lax.dot_general(
        a, b, (((1,), (1,)), ((), ())), precision=precision, preferred_element_type=F32
    )


def lanes(shape):
    return lax.broadcasted_iota(jnp.int32, shape, 1)


def rows(shape):
    return lax.broadcasted_iota(jnp.int32, shape, 0)


def by_halves(product, a, b):
    high = a.astype(BF16)
    low = (a - high.astype(F32)).astype(BF16)
    both = product(jnp.concatenate([high, low], axis=0), b, None)
    return both[: a.shape[0]] + both[a.shape[0] :]


def packed_product(left, right):
    return packed_rows(nt(left, jnp.concatenate([right, right], axis=0)))


def packed_rows(twice):
    upper, lower = twice[: M // 2], twice[M // 2 :]
    return jnp.where(lanes(upper.shape) < M, upper, lower)


def unpacked(packed):
    return jnp.concatenate([packed, pltpu.roll(packed, M, axis=1)], axis=0)


def factor(gram, out_ref):
    shape = (M, 2 * M)
    start = jnp.where(
        lanes(shape) < M, gram, jnp.where(lanes(shape) - M == rows(shape), 1.0, 0.0)
    )

    def four(matrix, s):
        c = [jnp.broadcast_to(matrix[:, s + i : s + i + 1], shape) for i in range(4)]
        r = [matrix[s + i : s + i + 1, :] for i in range(4)]
        p = [[c[j][s + i : s + i + 1, :] for j in range(4)] for i in range(4)]

        def pair(i):
            first, cross, last = p[i][i], p[i][i + 1], p[i + 1][i + 1]
            det = first * last - cross * cross
            root = lax.rsqrt(det)
            inverse = root * root
            scale = lax.rsqrt(first)
            upper = r[i] * scale
            lower = (r[i + 1] - r[i] * (cross * scale * scale)) * (root * first * scale)
            return last * inverse, -cross * inverse, first * inverse, [upper, lower]

        i00, i01, i11, done = pair(0)
        for i in (2, 3):
            w0 = p[0][i] * i00 + p[1][i] * i01
            w1 = p[0][i] * i01 + p[1][i] * i11
            r[i] = r[i] - w0 * r[0] - w1 * r[1]
            c[i] = c[i] - w0 * c[0] - w1 * c[1]
            for j in range(i, 4):
                p[i][j] = p[i][j] - w0 * p[0][j] - w1 * p[1][j]
        j00, j01, j11, more = pair(2)
        matrix = matrix - (
            c[0] * (i00 * r[0] + i01 * r[1])
            + c[1] * (i01 * r[0] + i11 * r[1])
            + c[2] * (j00 * r[2] + j01 * r[3])
            + c[3] * (j01 * r[2] + j11 * r[3])
        )
        return matrix, done + more

    def eight(block, matrix):
        matrix, done = four(matrix, 0)
        matrix, more = four(matrix, 4)
        finished = pltpu.roll(jnp.concatenate(done + more, axis=0), 8 * block, axis=1)
        out_ref[pl.ds(pl.multiple_of(8 * block, 8), 8), :] = finished
        matrix = jnp.concatenate([matrix[8:], matrix[:8]], axis=0)
        return pltpu.roll(matrix, 2 * M - 8, axis=1)

    lax.fori_loop(0, M // 8, eight, start)
    result = out_ref[...]
    upper = jnp.where(lanes(shape) >= rows(shape), result, 0.0)[:, :M]
    inverse = pltpu.roll(result, M, axis=1)[:, :M]
    return upper, inverse


def kernel(
    coarse_ref, corr_ref, near_ref, weight_ref, energy_ref, start_ref,
    residual_ref, coef_ref,
    cbuf, chalf, near_k, near_own, near_xy, near_z, near_xy_s, near_z_s, w_other, w_s,
    gk, gxy, gz, gsend, fac,
    ubuf, tbuf, ypart, ysend, yk, rsend, rbuf,
    uz, ak, asend, az, axy, afull, hk, hxy, hz, hsend,
    send, recv, local,
):
    row, col = lax.axis_index("row"), lax.axis_index("col")
    z, yh = row // 2, row % 2
    yl, x, k = col // 8, (col // 2) % 4, col % 2
    y = yh * 2 + yl
    me_xy = y * NX + x

    def device(x_, y_, z_, k_):
        return (z_ * 2 + y_ // 2, (y_ % 2) * 8 + x_ * 2 + k_)

    sibling = device(x, y, z, 1 - k)
    x_ring = [device((x + d) % NX, y, z, k) for d in range(1, NX)]
    y_ring = [device(x, (y + d) % NY, z, k) for d in range(1, NY)]
    z_ring = [device(x, y, (z + d) % NZ, k) for d in range(1, NZ)]
    plane = [
        device((x + dx) % NX, (y + dy) % NY, z, k)
        for dy in range(NY)
        for dx in range(NX)
        if dx or dy
    ]
    away = sorted(
        (min(dx, NX - dx) + min(dy, NY - dy), dx, dy) for dy in range(NY) for dx in range(NX)
    )
    near_to_far = [
        [(dx, dy) for hops, dx, dy in away if low <= hops <= high]
        for low, high in ((0, 0), (1, 1), (2, 2), (3, 4))
    ]
    count = [0]
    sent = []
    pending = []

    def push(src, dst, targets, like=None):
        i = count[0]
        count[0] += 1
        for d, target in enumerate(targets):
            pltpu.make_async_remote_copy(
                src_ref=src(d) if callable(src) else src, dst_ref=dst,
                send_sem=send.at[i], recv_sem=recv.at[i],
                device_id=target, device_id_type=MESH,
            ).start()
        like = dst if like is None else like
        sent.append((i, like))

        def wait():
            pltpu.make_async_copy(like, like, recv.at[i]).wait()
            pending.remove(wait)

        pending.append(wait)
        return wait

    barrier = pltpu.get_barrier_semaphore()
    partners = [sibling] + plane + z_ring
    for target in partners:
        pl.semaphore_signal(barrier, inc=1, device_id=target, device_id_type=MESH)
    near_own[...] = jnp.full((8, B), near_ref[0], jnp.int32)
    start_t = start_ref[...]
    gk[0] = packed_product(start_t, start_t)
    pl.semaphore_wait(barrier, len(partners))

    other_half = pl.ds(pl.multiple_of((1 - k) * 32, 32), 32)
    own_half = pl.ds(pl.multiple_of(k * 32, 32), 32)
    got_gk = push(gk.at[0], gk.at[1], [sibling])
    got_half = push(coarse_ref.at[other_half], chalf, [sibling])
    got_near_k = push(near_own, near_k, [sibling])
    corr = corr_ref[0]
    start_u = by_halves(nt, start_t, corr)

    got_gk()
    gxy[me_xy] = gk[0] + gk[1]
    got_gxy = push(gxy.at[me_xy], gxy.at[me_xy], plane, gxy.at[pl.ds(0, NXY - 1)])

    got_half()
    shape = (M, B)
    place_own = jnp.where(lanes(shape) == rows(shape) + M * k, 1.0, 0.0).astype(BF16)
    place_sib = jnp.where(lanes(shape) == rows(shape) + M * (1 - k), 1.0, 0.0).astype(BF16)
    strip = nn(coarse_ref[own_half, :], place_own, None) + nn(chalf[...], place_sib, None)
    cbuf[z, yl, x, yh, k] = strip.astype(BF16)
    mine = cbuf.at[z, yl, x, yh, k]
    got_a = push(mine, mine, z_ring, cbuf.at[pl.ds(0, 7), 0, 0, 0, 0])

    got_w = push(weight_ref, w_other, [y_ring[1]])
    near_xy[me_xy] = near_own[...]
    got_near_xy = push(near_xy.at[me_xy], near_xy.at[me_xy], plane, near_xy.at[pl.ds(0, NXY - 1)])
    got_near_k()
    near_z[z] = jnp.where(rows((8, B)) == 0, near_own[...], near_k[...])
    got_near_z = push(near_z.at[z], near_z.at[z], z_ring, near_z.at[pl.ds(0, NZ - 1)])

    got_a()
    b_first = cbuf.at[pl.ds(0, 4), yl, x, yh, k]
    b_second = cbuf.at[pl.ds(4, 4), yl, x, yh, k]
    twelve = cbuf.at[pl.ds(0, 6), :, 0, 0, 0]
    got_b1 = push(b_first, b_first, x_ring, twelve)
    got_b2 = push(b_second, b_second, y_ring, twelve)

    got_gxy()
    gz[z] = jnp.sum(gxy[...], axis=0)
    got_gz = push(gz.at[z], gz.at[z], z_ring, gz.at[pl.ds(0, NZ - 1)])

    def first_part(y_):
        return cbuf.at[pl.ds(0, 4), y_ % 2, :, y_ // 2, k]

    def second_part(x_):
        return cbuf.at[pl.ds(4, 4), :, x_, :, k]

    got_c, got_d = [], []
    got_b1()
    for d in (2, 1, 3):
        wait = push(first_part(y), first_part(y), [y_ring[d - 1]])
        got_c.insert(0, (wait, first_part((y - d) % NY)))
    got_b2()
    for d in (2, 1, 3):
        wait = push(second_part(x), second_part(x), [x_ring[d - 1]])
        got_c.insert(0, (wait, second_part((x - d) % NX)))
    got_c = [got_c[i] for i in (0, 1, 3, 4, 2, 5)]
    for part in (first_part(y), second_part(x)):
        got_d.append(push(part, part, [sibling]))

    got_w()
    got_near_xy()
    got_near_z()
    locals_ = [
        pltpu.make_async_copy(weight_ref, w_s.at[yh], local.at[0]),
        pltpu.make_async_copy(w_other, w_s.at[1 - yh], local.at[1]),
        pltpu.make_async_copy(near_xy, near_xy_s, local.at[2]),
        pltpu.make_async_copy(near_z, near_z_s, local.at[3]),
    ]
    for c in locals_:
        c.start()
        pending.append(c.wait)


    got_gz()
    gram = unpacked(jnp.sum(gz[...], axis=0) * (1.0 / TOTAL))
    _, inverse0 = factor(gram, fac.at[0])

    def gather(step, images):
        ubuf[step, me_xy] = images.astype(BF16)
        mine_ = ubuf.at[step, me_xy]
        waits = [None] * 3
        for g in (2, 1, 0):
            targets = [device((x + dx) % NX, (y + dy) % NY, z, k) for dx, dy in near_to_far[g + 1]]
            waits[g] = push(mine_, mine_, targets, ubuf.at[step, pl.ds(0, len(targets))])
        return waits

    got_u = gather(0, nn(inverse0, start_u))
    for wait, part in got_c:
        wait()
        got_d.append(push(part, part, [sibling]))
    for c in locals_:
        c.wait()
        pending.remove(c.wait)
    energy = energy_ref[...]
    basis = nn(inverse0, start_t)
    first_term = energy * basis
    first_term_u = by_halves(nt, first_term, corr)
    corr_gram = nt(corr, corr, None)
    corr_gram_high = corr_gram.astype(BF16)
    corr_gram_low = (corr_gram - corr_gram_high.astype(F32)).astype(BF16)
    for wait in got_d:
        wait()

    def distance(half, j):
        return j + 2 if half == 0 else jnp.where(j < 2, j + 6, 3 - j)

    got_r = {0: [], 1: []}

    def send_sums(step, half):
        targets = {0: (2, 3, 4, 5), 1: (6, 7, 1)}[half]
        first = 4 * half
        got_r[step].append(push(
            lambda i: rsend.at[step, first + i], rbuf.at[step, z],
            [z_ring[d - 1] for d in targets], rbuf.at[step, pl.ds(0, len(targets))],
        ))

    def apply(step, got_u, beside=None, between=None):
        def one_source(dx, dy):
            q = (y + dy) % NY * NX + (x + dx) % NX
            block = cbuf[near_xy_s[q, 0, 0]].reshape(8, B, B)
            vector = ubuf[step, q]
            for c in range(8):
                tbuf[q, c] = nn(vector, block[c], None)

        for g, group in enumerate(near_to_far):
            if g:
                got_u[g - 1]()
            for dx, dy in group:
                one_source(dx, dy)

        def target(d, other):
            z_ = (z + d) % NZ
            near = near_z_s[z_, other, 0]
            place = z_ * 32 + yh * 16 + yl * 8 + x * 2 + (1 - k if other else k)
            total = jnp.zeros((M, B), F32)
            for q in range(NXY):
                qy, qx = q // NX, q % NX
                w = w_s[qy // 2, (qy % 2) * 8 + qx * 2 + k, place]
                total = total + w * tbuf[q, near]
            return total

        got_yk = []
        for half in (0, 1):

            def for_sibling(j, _, half=half):
                ysend[step, 4 * half + j] = target(distance(half, j), 1)
                return 0

            lax.fori_loop(0, 4, for_sibling, 0)
            part = pl.ds(4 * half, 4)
            got_yk.append(push(ysend.at[step, part], yk.at[step, part], [sibling]))
        for half in (0, 1):

            def for_own(j, _, half=half):
                ypart[4 * half + j] = target(distance(half, j), 0)
                return 0

            lax.fori_loop(0, 4, for_own, 0)
            if half == 0 and beside is not None:
                beside()
            got_yk[half]()
            part = pl.ds(4 * half, 4)
            total = ypart[part] + yk[step, part]
            rsend[step, part] = total.astype(BF16)
            if half:
                own = total[3]
            if step == 0:
                send_sums(step, half)
        if step:
            between()
            send_sums(step, 0)
            send_sums(step, 1)
        rbuf[step, z] = jnp.zeros((M, B), BF16)

        def result():
            for wait in got_r[step]:
                wait()
            return own + jnp.sum(rbuf[step].astype(F32), axis=0)

        return result

    summed = apply(0, got_u)()
    high = summed.astype(BF16)
    low = (summed - high.astype(F32)).astype(BF16)
    twice = nn(jnp.concatenate([high, low], axis=0), corr_gram_high, None)
    image_u = first_term_u + (twice[:M] + twice[M:] + nn(high, corr_gram_low, None))
    got_u = gather(1, image_u)
    uz[z] = ubuf[1, me_xy]
    got_uz = push(uz.at[z], uz.at[z], z_ring, uz.at[pl.ds(0, NZ - 1)])
    image = first_term + by_halves(nn, summed, corr)
    ak[0] = nt(image, jnp.concatenate([basis, image], axis=0))
    got_ak = push(ak.at[0], ak.at[1], [sibling])
    energy_product = packed_product(image, energy * image)
    got_ak()
    asend[...] = (ak[0] + ak[1]).reshape(NZ, 8, B)
    az[z] = asend[z]
    got_az = push(
        lambda d: asend.at[(z + d + 1) % NZ], az.at[z], z_ring, az.at[pl.ds(0, NZ - 1)]
    )

    got_axy = []

    def beside():
        got_az()
        axy[me_xy] = jnp.sum(az[...], axis=0)
        got_axy.append(
            push(axy.at[me_xy], axy.at[me_xy], plane, axy.at[pl.ds(0, NXY - 1)])
        )

    got_hk = []

    def between():
        got_uz()
        images = jnp.concatenate(
            [uz[(z + d) % NZ] for d in (2, 3, 4, 5, 6, 7, 1, 0)], axis=1
        )
        sums = jnp.concatenate([rsend[1, i] for i in range(NZ)], axis=1)
        sums = jnp.concatenate([sums, sums], axis=0)
        hsend[...] = energy_product + packed_rows(nt(images, sums, None))
        got_hk.append(push(hsend, hk, [sibling]))

    second_sum = apply(1, got_u, beside, between)
    got_axy[0]()
    afull[z] = jnp.sum(axy[...], axis=0)
    got_afull = push(afull.at[z], afull.at[z], z_ring, afull.at[pl.ds(0, NZ - 1)])
    got_hk[0]()
    hxy[me_xy] = hsend[...] + hk[...]
    got_hxy = push(hxy.at[me_xy], hxy.at[me_xy], plane, hxy.at[pl.ds(0, NXY - 1)])
    image_sum = energy * image + by_halves(nn, second_sum(), corr)
    got_hxy()
    hz[z] = jnp.sum(hxy[...], axis=0)
    got_hz = push(hz.at[z], hz.at[z], z_ring, hz.at[pl.ds(0, NZ - 1)])
    got_afull()
    both = afull[...].reshape(M, B) * (1.0 / TOTAL)
    alpha_t = both[:, :M]
    square = pltpu.roll(both, M, axis=1)[:, :M]
    next_gram = square - nt(alpha_t, alpha_t)
    upper1, inverse1 = factor(jnp.concatenate([next_gram, next_gram], axis=1), fac.at[1])
    second = nn(inverse1, image - nn(alpha_t, basis))
    image_next = nn(inverse1, image_sum - nn(alpha_t, image)) - nn(upper1, basis)
    known = (
        nt(alpha_t, nn(alpha_t, alpha_t)) - nn(alpha_t, square) - nt(square, alpha_t)
    )
    coef_ref[0] = alpha_t
    coef_ref[1] = upper1
    across = lax.dot_general(
        inverse1, second, (((0,), (0,)), ((), ())), precision=HIGH, preferred_element_type=F32
    )
    got_hz()
    middle = unpacked(jnp.sum(hz[...], axis=0) * (1.0 / TOTAL))[:, :M] + known
    left = nn(inverse1, middle)
    residual_ref[...] = image_next - nn(left, across)
    coef_ref[2] = nt(left, inverse1)

    for i, like in sent:
        pltpu.make_async_copy(like, like, send.at[i]).wait()


def on_device(coarse_kernel, correlations, neighbor, pair_weight, energies, start_block):
    vmem = pl.BlockSpec(memory_space=pltpu.VMEM)
    smem = pl.BlockSpec(memory_space=pltpu.SMEM)
    residual_t, coefficients_t = pl.pallas_call(
        kernel,
        out_shape=(
            jax.ShapeDtypeStruct((M, B), F32),
            jax.ShapeDtypeStruct((3, M, M), F32),
        ),
        in_specs=[vmem, vmem, smem, vmem, vmem, vmem],
        out_specs=(vmem, vmem),
        scratch_shapes=[
            pltpu.VMEM((8, 2, 4, 2, 2, 32, B), BF16),
            pltpu.VMEM((32, M), BF16),
            pltpu.VMEM((8, B), jnp.int32),
            pltpu.VMEM((8, B), jnp.int32),
            pltpu.VMEM((NXY, 8, B), jnp.int32),
            pltpu.VMEM((NZ, 8, B), jnp.int32),
            pltpu.SMEM((NXY, 8, B), jnp.int32),
            pltpu.SMEM((NZ, 8, B), jnp.int32),
            pltpu.VMEM((16, 256), F32),
            pltpu.SMEM((2, 16, 256), F32),
            pltpu.VMEM((2, M // 2, B), F32),
            pltpu.VMEM((NXY, M // 2, B), F32),
            pltpu.VMEM((NZ, M // 2, B), F32),
            pltpu.VMEM((M // 2, B), F32),
            pltpu.VMEM((2, M, B), F32),
            pltpu.VMEM((2, NXY, M, B), BF16),
            pltpu.VMEM((NXY, 8, M, B), F32),
            pltpu.VMEM((NZ, M, B), F32),
            pltpu.VMEM((2, NZ, M, B), F32),
            pltpu.VMEM((2, NZ, M, B), F32),
            pltpu.VMEM((2, NZ, M, B), BF16),
            pltpu.VMEM((2, NZ, M, B), BF16),
            pltpu.VMEM((NZ, M, B), BF16),
            pltpu.VMEM((2, M, B), F32),
            pltpu.VMEM((NZ, 8, B), F32),
            pltpu.VMEM((NZ, 8, B), F32),
            pltpu.VMEM((NXY, 8, B), F32),
            pltpu.VMEM((NZ, 8, B), F32),
            pltpu.VMEM((M // 2, B), F32),
            pltpu.VMEM((NXY, M // 2, B), F32),
            pltpu.VMEM((NZ, M // 2, B), F32),
            pltpu.VMEM((M // 2, B), F32),
            pltpu.SemaphoreType.DMA((64,)),
            pltpu.SemaphoreType.DMA((64,)),
            pltpu.SemaphoreType.DMA((4,)),
        ],
        compiler_params=pltpu.CompilerParams(
            collective_id=0, has_side_effects=True, vmem_limit_bytes=40 << 20
        ),
    )(coarse_kernel, correlations, neighbor, pair_weight, energies.reshape(1, B), start_block.T)
    return residual_t.T, jnp.swapaxes(coefficients_t, 1, 2)


def solution(mesh):
    both = ("row", "col")
    return jax.shard_map(
        on_device,
        mesh=mesh,
        in_specs=(
            P("row", "col"),
            P(both, None, None),
            P(both),
            P("row", None),
            P(both),
            P(both, None),
        ),
        out_specs=(P(both, None), P()),
        check_vma=False,
    )
```

```python
import functools

import jax
import jax.numpy as jnp
from jax import lax
from jax.experimental import pallas as pl
from jax.experimental.pallas import tpu as pltpu
from jax.sharding import PartitionSpec as P

MESH = pl.DeviceIdType.MESH
HIGH = lax.Precision.HIGHEST
F32 = jnp.float32
BF16 = jnp.bfloat16
B = 128
M = 64
NX, NY, NZ = 4, 4, 8
NXY = NX * NY
TOTAL = 32768.0


def nn(a, b, precision=HIGH):
    return lax.dot_general(
        a, b, (((1,), (0,)), ((), ())), precision=precision, preferred_element_type=F32
    )


def nt(a, b, precision=HIGH):
    return lax.dot_general(
        a, b, (((1,), (1,)), ((), ())), precision=precision, preferred_element_type=F32
    )


def lanes(shape):
    return lax.broadcasted_iota(jnp.int32, shape, 1)


def rows(shape):
    return lax.broadcasted_iota(jnp.int32, shape, 0)


def by_halves(product, a, b):
    high = a.astype(BF16)
    low = (a - high.astype(F32)).astype(BF16)
    both = product(jnp.concatenate([high, low], axis=0), b, None)
    return both[: a.shape[0]] + both[a.shape[0] :]


def packed_product(left, right):
    return packed_rows(nt(left, jnp.concatenate([right, right], axis=0)))


def packed_rows(twice):
    upper, lower = twice[: M // 2], twice[M // 2 :]
    return jnp.where(lanes(upper.shape) < M, upper, lower)


def unpacked(packed):
    return jnp.concatenate([packed, pltpu.roll(packed, M, axis=1)], axis=0)


def factor(gram, out_ref):
    shape = (M, 2 * M)
    start = jnp.where(
        lanes(shape) < M, gram, jnp.where(lanes(shape) - M == rows(shape), 1.0, 0.0)
    )

    def four(matrix, s):
        c = [jnp.broadcast_to(matrix[:, s + i : s + i + 1], shape) for i in range(4)]
        r = [matrix[s + i : s + i + 1, :] for i in range(4)]
        p = [[c[j][s + i : s + i + 1, :] for j in range(4)] for i in range(4)]

        def pair(i):
            first, cross, last = p[i][i], p[i][i + 1], p[i + 1][i + 1]
            det = first * last - cross * cross
            root = lax.rsqrt(det)
            inverse = root * root
            scale = lax.rsqrt(first)
            upper = r[i] * scale
            lower = (r[i + 1] - r[i] * (cross * scale * scale)) * (root * first * scale)
            return last * inverse, -cross * inverse, first * inverse, [upper, lower]

        i00, i01, i11, done = pair(0)
        for i in (2, 3):
            w0 = p[0][i] * i00 + p[1][i] * i01
            w1 = p[0][i] * i01 + p[1][i] * i11
            r[i] = r[i] - w0 * r[0] - w1 * r[1]
            c[i] = c[i] - w0 * c[0] - w1 * c[1]
            for j in range(i, 4):
                p[i][j] = p[i][j] - w0 * p[0][j] - w1 * p[1][j]
        j00, j01, j11, more = pair(2)
        matrix = matrix - (
            c[0] * (i00 * r[0] + i01 * r[1])
            + c[1] * (i01 * r[0] + i11 * r[1])
            + c[2] * (j00 * r[2] + j01 * r[3])
            + c[3] * (j01 * r[2] + j11 * r[3])
        )
        return matrix, done + more

    def eight(block, matrix):
        matrix, done = four(matrix, 0)
        matrix, more = four(matrix, 4)
        finished = pltpu.roll(jnp.concatenate(done + more, axis=0), 8 * block, axis=1)
        out_ref[pl.ds(pl.multiple_of(8 * block, 8), 8), :] = finished
        matrix = jnp.concatenate([matrix[8:], matrix[:8]], axis=0)
        return pltpu.roll(matrix, 2 * M - 8, axis=1)

    lax.fori_loop(0, M // 8, eight, start)
    result = out_ref[...]
    upper = jnp.where(lanes(shape) >= rows(shape), result, 0.0)[:, :M]
    inverse = pltpu.roll(result, M, axis=1)[:, :M]
    return upper, inverse


def kernel(
    coarse_in, corr_in, near_ref, weight_in, energy_in, start_in,
    residual_ref, coef_ref,
    coarse_ref, corr_ref, weight_ref, energy_ref, start_ref,
    cbuf, chalf, near_k, near_own, near_xy, near_z, near_xy_s, near_z_s, w_other, w_s,
    gk, gxy, gz, gsend, fac,
    ubuf, tbuf, ypart, ysend, yk, rsend, rbuf,
    uz, ak, asend, az, axy, afull, hk, hxy, hz, hsend,
    send, recv, local,
):
    row, col = lax.axis_index("row"), lax.axis_index("col")
    z, yh = row // 2, row % 2
    yl, x, k = col // 8, (col // 2) % 4, col % 2
    y = yh * 2 + yl
    me_xy = y * NX + x

    def device(x_, y_, z_, k_):
        return (z_ * 2 + y_ // 2, (y_ % 2) * 8 + x_ * 2 + k_)

    sibling = device(x, y, z, 1 - k)
    x_ring = [device((x + d) % NX, y, z, k) for d in range(1, NX)]
    y_ring = [device(x, (y + d) % NY, z, k) for d in range(1, NY)]
    z_ring = [device(x, y, (z + d) % NZ, k) for d in range(1, NZ)]
    plane = [
        device((x + dx) % NX, (y + dy) % NY, z, k)
        for dy in range(NY)
        for dx in range(NX)
        if dx or dy
    ]
    away = sorted(
        (min(dx, NX - dx) + min(dy, NY - dy), dx, dy) for dy in range(NY) for dx in range(NX)
    )
    near_to_far = [
        [(dx, dy) for hops, dx, dy in away if low <= hops <= high]
        for low, high in ((0, 0), (1, 1), (2, 2), (3, 4))
    ]
    count = [0]
    sent = []
    pending = []

    def push(src, dst, targets, like=None):
        i = count[0]
        count[0] += 1
        for d, target in enumerate(targets):
            pltpu.make_async_remote_copy(
                src_ref=src(d) if callable(src) else src, dst_ref=dst,
                send_sem=send.at[i], recv_sem=recv.at[i],
                device_id=target, device_id_type=MESH,
            ).start()
        like = dst if like is None else like
        sent.append((i, like))

        def wait():
            pltpu.make_async_copy(like, like, recv.at[i]).wait()
            pending.remove(wait)

        pending.append(wait)
        return wait

    loads = [
        pltpu.make_async_copy(source, place, local.at[4 + i])
        for i, (source, place) in enumerate((
            (start_in, start_ref), (coarse_in, coarse_ref), (corr_in, corr_ref),
            (weight_in, weight_ref), (energy_in, energy_ref),
        ))
    ]
    for load in loads:
        load.start()
    barrier = pltpu.get_barrier_semaphore()
    partners = [sibling] + plane + z_ring
    for target in partners:
        pl.semaphore_signal(barrier, inc=1, device_id=target, device_id_type=MESH)
    near_own[...] = jnp.full((8, B), near_ref[0], jnp.int32)
    loads[0].wait()
    start_t = start_ref[...]
    gk[0] = packed_product(start_t, start_t)
    for load in loads[1:]:
        load.wait()
    pl.semaphore_wait(barrier, len(partners))

    other_half = pl.ds(pl.multiple_of((1 - k) * 32, 32), 32)
    own_half = pl.ds(pl.multiple_of(k * 32, 32), 32)
    got_gk = push(gk.at[0], gk.at[1], [sibling])
    got_half = push(coarse_ref.at[other_half], chalf, [sibling])
    got_near_k = push(near_own, near_k, [sibling])
    corr = corr_ref[0]
    start_u = by_halves(nt, start_t, corr)

    got_gk()
    gxy[me_xy] = gk[0] + gk[1]
    got_gxy = push(gxy.at[me_xy], gxy.at[me_xy], plane, gxy.at[pl.ds(0, NXY - 1)])

    got_half()
    shape = (M, B)
    place_own = jnp.where(lanes(shape) == rows(shape) + M * k, 1.0, 0.0).astype(BF16)
    place_sib = jnp.where(lanes(shape) == rows(shape) + M * (1 - k), 1.0, 0.0).astype(BF16)
    strip = nn(coarse_ref[own_half, :], place_own, None) + nn(chalf[...], place_sib, None)
    cbuf[z, yl, x, yh, k] = strip.astype(BF16)
    mine = cbuf.at[z, yl, x, yh, k]
    got_a = push(mine, mine, z_ring, cbuf.at[pl.ds(0, 7), 0, 0, 0, 0])

    got_w = push(weight_ref, w_other, [y_ring[1]])
    near_xy[me_xy] = near_own[...]
    got_near_xy = push(near_xy.at[me_xy], near_xy.at[me_xy], plane, near_xy.at[pl.ds(0, NXY - 1)])
    got_near_k()
    near_z[z] = jnp.where(rows((8, B)) == 0, near_own[...], near_k[...])
    got_near_z = push(near_z.at[z], near_z.at[z], z_ring, near_z.at[pl.ds(0, NZ - 1)])

    got_a()
    b_first = cbuf.at[pl.ds(0, 4), yl, x, yh, k]
    b_second = cbuf.at[pl.ds(4, 4), yl, x, yh, k]
    twelve = cbuf.at[pl.ds(0, 6), :, 0, 0, 0]
    got_b1 = push(b_first, b_first, x_ring, twelve)
    got_b2 = push(b_second, b_second, y_ring, twelve)

    got_gxy()
    gz[z] = jnp.sum(gxy[...], axis=0)
    got_gz = push(gz.at[z], gz.at[z], z_ring, gz.at[pl.ds(0, NZ - 1)])

    def first_part(y_):
        return cbuf.at[pl.ds(0, 4), y_ % 2, :, y_ // 2, k]

    def second_part(x_):
        return cbuf.at[pl.ds(4, 4), :, x_, :, k]

    got_c, got_d = [], []
    got_b1()
    for d in (1, 3, 2):
        wait = push(first_part(y), first_part(y), [y_ring[d - 1]])
        got_c.append((d, wait, first_part((y - d) % NY)))
    got_b2()
    for d in (1, 3, 2):
        wait = push(second_part(x), second_part(x), [x_ring[d - 1]])
        got_c.append((d, wait, second_part((x - d) % NX)))
    got_c = [(wait, part) for d, wait, part in sorted(got_c, key=lambda e: e[0] == 2)]
    for part in (first_part(y), second_part(x)):
        got_d.append(push(part, part, [sibling]))

    got_w()
    got_near_xy()
    got_near_z()
    locals_ = [
        pltpu.make_async_copy(weight_ref, w_s.at[yh], local.at[0]),
        pltpu.make_async_copy(w_other, w_s.at[1 - yh], local.at[1]),
        pltpu.make_async_copy(near_xy, near_xy_s, local.at[2]),
        pltpu.make_async_copy(near_z, near_z_s, local.at[3]),
    ]
    for c in locals_:
        c.start()
        pending.append(c.wait)


    got_gz()
    gram = unpacked(jnp.sum(gz[...], axis=0) * (1.0 / TOTAL))
    _, inverse0 = factor(gram, fac.at[0])

    def gather(step, images):
        ubuf[step, me_xy] = images.astype(BF16)
        mine_ = ubuf.at[step, me_xy]
        waits = [None] * 3
        for g in (2, 1, 0):
            targets = [device((x + dx) % NX, (y + dy) % NY, z, k) for dx, dy in near_to_far[g + 1]]
            waits[g] = push(mine_, mine_, targets, ubuf.at[step, pl.ds(0, len(targets))])
        return waits

    got_u = gather(0, nn(inverse0, start_u))
    for wait, part in got_c:
        wait()
        got_d.append(push(part, part, [sibling]))
    for c in locals_:
        c.wait()
        pending.remove(c.wait)
    energy = energy_ref[...]
    basis = nn(inverse0, start_t)
    first_term = energy * basis
    first_term_u = by_halves(nt, first_term, corr)
    corr_gram = nt(corr, corr, None)
    corr_gram_high = corr_gram.astype(BF16)
    corr_gram_low = (corr_gram - corr_gram_high.astype(F32)).astype(BF16)
    for wait in got_d:
        wait()

    def distance(half, j):
        return j + 2 if half == 0 else jnp.where(j < 2, j + 6, 3 - j)

    got_r = {0: [], 1: []}

    def send_sums(step, half):
        targets = {0: (2, 3, 4, 5), 1: (6, 7, 1)}[half]
        first = 4 * half
        got_r[step].append(push(
            lambda i: rsend.at[step, first + i], rbuf.at[step, z],
            [z_ring[d - 1] for d in targets], rbuf.at[step, pl.ds(0, len(targets))],
        ))

    def apply(step, got_u, beside=None, between=None):
        def one_source(dx, dy):
            q = (y + dy) % NY * NX + (x + dx) % NX
            block = cbuf[near_xy_s[q, 0, 0]].reshape(8, B, B)
            vector = ubuf[step, q]
            for c in range(8):
                tbuf[q, c] = nn(vector, block[c], None)

        for g, group in enumerate(near_to_far):
            if g:
                got_u[g - 1]()
            for dx, dy in group:
                one_source(dx, dy)

        def target(d, other):
            z_ = (z + d) % NZ
            near = near_z_s[z_, other, 0]
            place = z_ * 32 + yh * 16 + yl * 8 + x * 2 + (1 - k if other else k)
            total = jnp.zeros((M, B), F32)
            for q in range(NXY):
                qy, qx = q // NX, q % NX
                w = w_s[qy // 2, (qy % 2) * 8 + qx * 2 + k, place]
                total = total + w * tbuf[q, near]
            return total

        got_yk = []
        for half in (0, 1):

            def for_sibling(j, _, half=half):
                ysend[step, 4 * half + j] = target(distance(half, j), 1)
                return 0

            lax.fori_loop(0, 4, for_sibling, 0)
            part = pl.ds(4 * half, 4)
            got_yk.append(push(ysend.at[step, part], yk.at[step, part], [sibling]))
        for half in (0, 1):

            def for_own(j, _, half=half):
                ypart[4 * half + j] = target(distance(half, j), 0)
                return 0

            lax.fori_loop(0, 4, for_own, 0)
            if half == 0 and beside is not None:
                beside()
            got_yk[half]()
            part = pl.ds(4 * half, 4)
            total = ypart[part] + yk[step, part]
            rsend[step, part] = total.astype(BF16)
            if half:
                own = total[3]
            if step == 0:
                send_sums(step, half)
        if step:
            between()
            send_sums(step, 0)
            send_sums(step, 1)
        rbuf[step, z] = jnp.zeros((M, B), BF16)

        def result():
            for wait in got_r[step]:
                wait()
            return own + jnp.sum(rbuf[step].astype(F32), axis=0)

        return result

    summed = apply(0, got_u)()
    high = summed.astype(BF16)
    low = (summed - high.astype(F32)).astype(BF16)
    twice = nn(jnp.concatenate([high, low], axis=0), corr_gram_high, None)
    image_u = first_term_u + (twice[:M] + twice[M:] + nn(high, corr_gram_low, None))
    got_u = gather(1, image_u)
    uz[z] = ubuf[1, me_xy]
    got_uz = push(uz.at[z], uz.at[z], z_ring, uz.at[pl.ds(0, NZ - 1)])
    image = first_term + by_halves(nn, summed, corr)
    ak[0] = nt(image, jnp.concatenate([basis, image], axis=0))
    got_ak = push(ak.at[0], ak.at[1], [sibling])
    energy_product = packed_product(image, energy * image)
    got_ak()
    asend[...] = (ak[0] + ak[1]).reshape(NZ, 8, B)
    az[z] = asend[z]
    got_az = push(
        lambda d: asend.at[(z + d + 1) % NZ], az.at[z], z_ring, az.at[pl.ds(0, NZ - 1)]
    )

    got_axy = []

    def beside():
        got_az()
        axy[me_xy] = jnp.sum(az[...], axis=0)
        got_axy.append(
            push(axy.at[me_xy], axy.at[me_xy], plane, axy.at[pl.ds(0, NXY - 1)])
        )

    got_hk = []

    def between():
        got_uz()
        images = jnp.concatenate(
            [uz[(z + d) % NZ] for d in (2, 3, 4, 5, 6, 7, 1, 0)], axis=1
        )
        sums = jnp.concatenate([rsend[1, i] for i in range(NZ)], axis=1)
        sums = jnp.concatenate([sums, sums], axis=0)
        hsend[...] = energy_product + packed_rows(nt(images, sums, None))
        got_hk.append(push(hsend, hk, [sibling]))

    second_sum = apply(1, got_u, beside, between)
    got_axy[0]()
    afull[z] = jnp.sum(axy[...], axis=0)
    got_afull = push(afull.at[z], afull.at[z], z_ring, afull.at[pl.ds(0, NZ - 1)])
    got_hk[0]()
    hxy[me_xy] = hsend[...] + hk[...]
    got_hxy = push(hxy.at[me_xy], hxy.at[me_xy], plane, hxy.at[pl.ds(0, NXY - 1)])
    image_sum = energy * image + by_halves(nn, second_sum(), corr)
    got_hxy()
    hz[z] = jnp.sum(hxy[...], axis=0)
    got_hz = push(hz.at[z], hz.at[z], z_ring, hz.at[pl.ds(0, NZ - 1)])
    got_afull()
    both = afull[...].reshape(M, B) * (1.0 / TOTAL)
    alpha_t = both[:, :M]
    square = pltpu.roll(both, M, axis=1)[:, :M]
    next_gram = square - nt(alpha_t, alpha_t)
    upper1, inverse1 = factor(jnp.concatenate([next_gram, next_gram], axis=1), fac.at[1])
    second = nn(inverse1, image - nn(alpha_t, basis))
    image_next = nn(inverse1, image_sum - nn(alpha_t, image)) - nn(upper1, basis)
    known = (
        nt(alpha_t, nn(alpha_t, alpha_t)) - nn(alpha_t, square) - nt(square, alpha_t)
    )
    coef_ref[0] = alpha_t
    coef_ref[1] = upper1
    across = lax.dot_general(
        inverse1, second, (((0,), (0,)), ((), ())), precision=HIGH, preferred_element_type=F32
    )
    got_hz()
    middle = unpacked(jnp.sum(hz[...], axis=0) * (1.0 / TOTAL))[:, :M] + known
    left = nn(inverse1, middle)
    residual_ref[...] = image_next - nn(left, across)
    coef_ref[2] = nt(left, inverse1)

    for i, like in sent:
        pltpu.make_async_copy(like, like, send.at[i]).wait()


def hand_over(residual_ref, coef_ref, residual_out, coef_out):
    residual_out[...] = residual_ref[...]
    for i in range(3):
        coef_out[i] = coef_ref[i].T


def on_device(coarse_kernel, correlations, neighbor, pair_weight, energies, start_block):
    vmem = pl.BlockSpec(memory_space=pltpu.VMEM)
    smem = pl.BlockSpec(memory_space=pltpu.SMEM)
    hbm = pl.BlockSpec(memory_space=pltpu.HBM)
    residual_t, coefficients_t = pl.pallas_call(
        kernel,
        out_shape=(
            jax.ShapeDtypeStruct((M, B), F32),
            jax.ShapeDtypeStruct((3, M, M), F32),
        ),
        in_specs=[hbm, hbm, smem, hbm, hbm, hbm],
        out_specs=(vmem, vmem),
        scratch_shapes=[
            pltpu.VMEM((M, M), BF16),
            pltpu.VMEM((1, B, B), BF16),
            pltpu.VMEM((16, 256), F32),
            pltpu.VMEM((1, B), F32),
            pltpu.VMEM((M, B), F32),
            pltpu.VMEM((8, 2, 4, 2, 2, 32, B), BF16),
            pltpu.VMEM((32, M), BF16),
            pltpu.VMEM((8, B), jnp.int32),
            pltpu.VMEM((8, B), jnp.int32),
            pltpu.VMEM((NXY, 8, B), jnp.int32),
            pltpu.VMEM((NZ, 8, B), jnp.int32),
            pltpu.SMEM((NXY, 8, B), jnp.int32),
            pltpu.SMEM((NZ, 8, B), jnp.int32),
            pltpu.VMEM((16, 256), F32),
            pltpu.SMEM((2, 16, 256), F32),
            pltpu.VMEM((2, M // 2, B), F32),
            pltpu.VMEM((NXY, M // 2, B), F32),
            pltpu.VMEM((NZ, M // 2, B), F32),
            pltpu.VMEM((M // 2, B), F32),
            pltpu.VMEM((2, M, B), F32),
            pltpu.VMEM((2, NXY, M, B), BF16),
            pltpu.VMEM((NXY, 8, M, B), F32),
            pltpu.VMEM((NZ, M, B), F32),
            pltpu.VMEM((2, NZ, M, B), F32),
            pltpu.VMEM((2, NZ, M, B), F32),
            pltpu.VMEM((2, NZ, M, B), BF16),
            pltpu.VMEM((2, NZ, M, B), BF16),
            pltpu.VMEM((NZ, M, B), BF16),
            pltpu.VMEM((2, M, B), F32),
            pltpu.VMEM((NZ, 8, B), F32),
            pltpu.VMEM((NZ, 8, B), F32),
            pltpu.VMEM((NXY, 8, B), F32),
            pltpu.VMEM((NZ, 8, B), F32),
            pltpu.VMEM((M // 2, B), F32),
            pltpu.VMEM((NXY, M // 2, B), F32),
            pltpu.VMEM((NZ, M // 2, B), F32),
            pltpu.VMEM((M // 2, B), F32),
            pltpu.SemaphoreType.DMA((64,)),
            pltpu.SemaphoreType.DMA((64,)),
            pltpu.SemaphoreType.DMA((9,)),
        ],
        compiler_params=pltpu.CompilerParams(
            collective_id=0, has_side_effects=True, vmem_limit_bytes=60 << 20
        ),
    )(coarse_kernel, correlations, neighbor, pair_weight, energies.reshape(1, B), start_block.T)
    residual_t, coefficients = pl.pallas_call(
        hand_over,
        out_shape=(
            jax.ShapeDtypeStruct((M, B), F32),
            jax.ShapeDtypeStruct((3, M, M), F32),
        ),
        in_specs=[vmem, vmem],
        out_specs=(vmem, vmem),
    )(residual_t, coefficients_t)
    return residual_t.T, coefficients


def solution(mesh):
    both = ("row", "col")
    return jax.shard_map(
        on_device,
        mesh=mesh,
        in_specs=(
            P("row", "col"),
            P(both, None, None),
            P(both),
            P("row", None),
            P(both),
            P(both, None),
        ),
        out_specs=(P(both, None), P()),
        check_vma=False,
    )
```

```python
import functools

import jax
import jax.numpy as jnp
from jax import lax
from jax.experimental import pallas as pl
from jax.experimental.pallas import tpu as pltpu
from jax.sharding import PartitionSpec as P

MESH = pl.DeviceIdType.MESH
HIGH = lax.Precision.HIGHEST
F32 = jnp.float32
BF16 = jnp.bfloat16
B = 128
M = 64
NX, NY, NZ = 4, 4, 8
NXY = NX * NY
TOTAL = 32768.0


def nn(a, b, precision=HIGH):
    return lax.dot_general(
        a, b, (((1,), (0,)), ((), ())), precision=precision, preferred_element_type=F32
    )


def nt(a, b, precision=HIGH):
    return lax.dot_general(
        a, b, (((1,), (1,)), ((), ())), precision=precision, preferred_element_type=F32
    )


def lanes(shape):
    return lax.broadcasted_iota(jnp.int32, shape, 1)


def rows(shape):
    return lax.broadcasted_iota(jnp.int32, shape, 0)


def by_halves(product, a, b):
    high = a.astype(BF16)
    low = (a - high.astype(F32)).astype(BF16)
    both = product(jnp.concatenate([high, low], axis=0), b, None)
    return both[: a.shape[0]] + both[a.shape[0] :]


def packed_product(left, right):
    return packed_rows(nt(left, jnp.concatenate([right, right], axis=0)))


def packed_rows(twice):
    upper, lower = twice[: M // 2], twice[M // 2 :]
    return jnp.where(lanes(upper.shape) < M, upper, lower)


def unpacked(packed):
    return jnp.concatenate([packed, pltpu.roll(packed, M, axis=1)], axis=0)


def factor(gram, out_ref):
    shape = (M, 2 * M)
    start = jnp.where(
        lanes(shape) < M, gram, jnp.where(lanes(shape) - M == rows(shape), 1.0, 0.0)
    )

    def four(matrix, s):
        c = [jnp.broadcast_to(matrix[:, s + i : s + i + 1], shape) for i in range(4)]
        r = [matrix[s + i : s + i + 1, :] for i in range(4)]
        p = [[c[j][s + i : s + i + 1, :] for j in range(4)] for i in range(4)]

        def pair(i):
            first, cross, last = p[i][i], p[i][i + 1], p[i + 1][i + 1]
            det = first * last - cross * cross
            root = lax.rsqrt(det)
            inverse = root * root
            scale = lax.rsqrt(first)
            upper = r[i] * scale
            lower = (r[i + 1] - r[i] * (cross * scale * scale)) * (root * first * scale)
            return last * inverse, -cross * inverse, first * inverse, [upper, lower]

        i00, i01, i11, done = pair(0)
        for i in (2, 3):
            w0 = p[0][i] * i00 + p[1][i] * i01
            w1 = p[0][i] * i01 + p[1][i] * i11
            r[i] = r[i] - w0 * r[0] - w1 * r[1]
            c[i] = c[i] - w0 * c[0] - w1 * c[1]
            for j in range(i, 4):
                p[i][j] = p[i][j] - w0 * p[0][j] - w1 * p[1][j]
        j00, j01, j11, more = pair(2)
        matrix = matrix - (
            c[0] * (i00 * r[0] + i01 * r[1])
            + c[1] * (i01 * r[0] + i11 * r[1])
            + c[2] * (j00 * r[2] + j01 * r[3])
            + c[3] * (j01 * r[2] + j11 * r[3])
        )
        return matrix, done + more

    def eight(block, matrix):
        matrix, done = four(matrix, 0)
        matrix, more = four(matrix, 4)
        finished = pltpu.roll(jnp.concatenate(done + more, axis=0), 8 * block, axis=1)
        out_ref[pl.ds(pl.multiple_of(8 * block, 8), 8), :] = finished
        matrix = jnp.concatenate([matrix[8:], matrix[:8]], axis=0)
        return pltpu.roll(matrix, 2 * M - 8, axis=1)

    lax.fori_loop(0, M // 8, eight, start)
    result = out_ref[...]
    upper = jnp.where(lanes(shape) >= rows(shape), result, 0.0)[:, :M]
    inverse = pltpu.roll(result, M, axis=1)[:, :M]
    return upper, inverse


def kernel(
    coarse_in, corr_in, near_ref, weight_in, energy_in, start_in,
    residual_ref, coef_ref,
    coarse_ref, corr_ref, weight_ref, energy_ref, start_ref,
    cbuf, chalf, near_k, near_own, near_xy, near_z, near_xy_s, near_z_s, w_other, w_s,
    gk, gxy, gz, gsend, fac,
    ubuf, tbuf, ypart, ysend, yk, rsend, rbuf,
    uz, ak, asend, az, axy, afull, hk, hxy, hz, hsend,
    send, recv, local,
):
    row, col = lax.axis_index("row"), lax.axis_index("col")
    z, yh = row // 2, row % 2
    yl, x, k = col // 8, (col // 2) % 4, col % 2
    y = yh * 2 + yl
    me_xy = y * NX + x

    def device(x_, y_, z_, k_):
        return (z_ * 2 + y_ // 2, (y_ % 2) * 8 + x_ * 2 + k_)

    sibling = device(x, y, z, 1 - k)
    x_ring = [device((x + d) % NX, y, z, k) for d in range(1, NX)]
    y_ring = [device(x, (y + d) % NY, z, k) for d in range(1, NY)]
    z_ring = [device(x, y, (z + d) % NZ, k) for d in range(1, NZ)]
    plane = [
        device((x + dx) % NX, (y + dy) % NY, z, k)
        for dy in range(NY)
        for dx in range(NX)
        if dx or dy
    ]
    away = sorted(
        (min(dx, NX - dx) + min(dy, NY - dy), dx, dy) for dy in range(NY) for dx in range(NX)
    )
    near_to_far = [
        [(dx, dy) for hops, dx, dy in away if low <= hops <= high]
        for low, high in ((0, 0), (1, 1), (2, 2), (3, 4))
    ]
    plane_far = [
        device((x + dx) % NX, (y + dy) % NY, z, k) for hops, dx, dy in away[::-1] if hops
    ]
    z_far = [z_ring[d - 1] for d in (4, 3, 5, 2, 6, 1, 7)]
    count = [0]
    sent = []
    pending = []

    def push(src, dst, targets, like=None):
        i = count[0]
        count[0] += 1
        for d, target in enumerate(targets):
            pltpu.make_async_remote_copy(
                src_ref=src(d) if callable(src) else src, dst_ref=dst,
                send_sem=send.at[i], recv_sem=recv.at[i],
                device_id=target, device_id_type=MESH,
            ).start()
        like = dst if like is None else like
        sent.append((i, like))

        def wait():
            pltpu.make_async_copy(like, like, recv.at[i]).wait()
            pending.remove(wait)

        pending.append(wait)
        return wait

    loads = [
        pltpu.make_async_copy(source, place, local.at[4 + i])
        for i, (source, place) in enumerate((
            (start_in, start_ref), (coarse_in, coarse_ref), (corr_in, corr_ref),
            (weight_in, weight_ref), (energy_in, energy_ref),
        ))
    ]
    for load in loads:
        load.start()
    barrier = pltpu.get_barrier_semaphore()
    partners = [sibling] + plane + z_ring
    for target in partners:
        pl.semaphore_signal(barrier, inc=1, device_id=target, device_id_type=MESH)
    near_own[...] = jnp.full((8, B), near_ref[0], jnp.int32)
    loads[0].wait()
    start_t = start_ref[...]
    gk[0] = packed_product(start_t, start_t)
    for load in loads[1:]:
        load.wait()
    pl.semaphore_wait(barrier, len(partners))

    other_half = pl.ds(pl.multiple_of((1 - k) * 32, 32), 32)
    own_half = pl.ds(pl.multiple_of(k * 32, 32), 32)
    got_gk = push(gk.at[0], gk.at[1], [sibling])
    got_half = push(coarse_ref.at[other_half], chalf, [sibling])
    got_near_k = push(near_own, near_k, [sibling])
    corr = corr_ref[0]
    start_u = by_halves(nt, start_t, corr)

    got_gk()
    gxy[me_xy] = gk[0] + gk[1]
    got_gxy = push(gxy.at[me_xy], gxy.at[me_xy], plane_far, gxy.at[pl.ds(0, NXY - 1)])

    got_half()
    shape = (M, B)
    place_own = jnp.where(lanes(shape) == rows(shape) + M * k, 1.0, 0.0).astype(BF16)
    place_sib = jnp.where(lanes(shape) == rows(shape) + M * (1 - k), 1.0, 0.0).astype(BF16)
    strip = nn(coarse_ref[own_half, :], place_own, None) + nn(chalf[...], place_sib, None)
    cbuf[z, yl, x, yh, k] = strip.astype(BF16)
    mine = cbuf.at[z, yl, x, yh, k]
    got_a = push(mine, mine, z_far, cbuf.at[pl.ds(0, 7), 0, 0, 0, 0])

    got_w = push(weight_ref, w_other, [y_ring[1]])
    near_xy[me_xy] = near_own[...]
    got_near_xy = push(near_xy.at[me_xy], near_xy.at[me_xy], plane_far, near_xy.at[pl.ds(0, NXY - 1)])
    got_near_k()
    near_z[z] = jnp.where(rows((8, B)) == 0, near_own[...], near_k[...])
    got_near_z = push(near_z.at[z], near_z.at[z], z_far, near_z.at[pl.ds(0, NZ - 1)])

    got_a()
    b_first = cbuf.at[pl.ds(0, 4), yl, x, yh, k]
    b_second = cbuf.at[pl.ds(4, 4), yl, x, yh, k]
    twelve = cbuf.at[pl.ds(0, 6), :, 0, 0, 0]
    got_b1 = push(b_first, b_first, x_ring, twelve)
    got_b2 = push(b_second, b_second, y_ring, twelve)

    got_gxy()
    gz[z] = jnp.sum(gxy[...], axis=0)
    got_gz = push(gz.at[z], gz.at[z], z_far, gz.at[pl.ds(0, NZ - 1)])

    def first_part(y_):
        return cbuf.at[pl.ds(0, 4), y_ % 2, :, y_ // 2, k]

    def second_part(x_):
        return cbuf.at[pl.ds(4, 4), :, x_, :, k]

    got_c, got_d = [], []
    got_b1()
    for d in (1, 3, 2):
        wait = push(first_part(y), first_part(y), [y_ring[d - 1]])
        got_c.append((d, wait, first_part((y - d) % NY)))
    got_b2()
    for d in (1, 3, 2):
        wait = push(second_part(x), second_part(x), [x_ring[d - 1]])
        got_c.append((d, wait, second_part((x - d) % NX)))
    got_c = [(wait, part) for d, wait, part in sorted(got_c, key=lambda e: e[0] == 2)]
    for part in (first_part(y), second_part(x)):
        got_d.append(push(part, part, [sibling]))

    got_w()
    got_near_xy()
    got_near_z()
    locals_ = [
        pltpu.make_async_copy(weight_ref, w_s.at[yh], local.at[0]),
        pltpu.make_async_copy(w_other, w_s.at[1 - yh], local.at[1]),
        pltpu.make_async_copy(near_xy, near_xy_s, local.at[2]),
        pltpu.make_async_copy(near_z, near_z_s, local.at[3]),
    ]
    for c in locals_:
        c.start()
        pending.append(c.wait)


    got_gz()
    gram = unpacked(jnp.sum(gz[...], axis=0) * (1.0 / TOTAL))
    _, inverse0 = factor(gram, fac.at[0])

    def gather(step, images):
        ubuf[step, me_xy] = images.astype(BF16)
        mine_ = ubuf.at[step, me_xy]
        waits = [None] * 3
        for g in (2, 1, 0):
            targets = [device((x + dx) % NX, (y + dy) % NY, z, k) for dx, dy in near_to_far[g + 1]]
            waits[g] = push(mine_, mine_, targets, ubuf.at[step, pl.ds(0, len(targets))])
        return waits

    got_u = gather(0, nn(inverse0, start_u))
    for wait, part in got_c:
        wait()
        got_d.append(push(part, part, [sibling]))
    for c in locals_:
        c.wait()
        pending.remove(c.wait)
    energy = energy_ref[...]
    basis = nn(inverse0, start_t)
    first_term = energy * basis
    first_term_u = by_halves(nt, first_term, corr)
    corr_gram = nt(corr, corr, None)
    corr_gram_high = corr_gram.astype(BF16)
    corr_gram_low = (corr_gram - corr_gram_high.astype(F32)).astype(BF16)
    for wait in got_d:
        wait()

    def distance(half, j):
        return j + 2 if half == 0 else jnp.where(j < 2, j + 6, 3 - j)

    got_r = {0: [], 1: []}

    def send_sums(step, half):
        entries = {0: (2, 1, 3, 0), 1: (4, 5, 6)}[half]
        targets = {0: (4, 3, 5, 2), 1: (6, 7, 1)}[half]
        got_r[step].append(push(
            lambda i: rsend.at[step, entries[i]], rbuf.at[step, z],
            [z_ring[d - 1] for d in targets], rbuf.at[step, pl.ds(0, len(targets))],
        ))

    def apply(step, got_u, beside=None, between=None):
        def one_source(dx, dy):
            q = (y + dy) % NY * NX + (x + dx) % NX
            block = cbuf[near_xy_s[q, 0, 0]].reshape(8, B, B)
            vector = ubuf[step, q]
            for c in range(8):
                tbuf[q, c] = nn(vector, block[c], None)

        for g, group in enumerate(near_to_far):
            if g:
                got_u[g - 1]()
            for dx, dy in group:
                one_source(dx, dy)

        def target(d, other):
            z_ = (z + d) % NZ
            near = near_z_s[z_, other, 0]
            place = z_ * 32 + yh * 16 + yl * 8 + x * 2 + (1 - k if other else k)
            total = jnp.zeros((M, B), F32)
            for q in range(NXY):
                qy, qx = q // NX, q % NX
                w = w_s[qy // 2, (qy % 2) * 8 + qx * 2 + k, place]
                total = total + w * tbuf[q, near]
            return total

        got_yk = []
        for half in (0, 1):

            def for_sibling(j, _, half=half):
                ysend[step, 4 * half + j] = target(distance(half, j), 1)
                return 0

            lax.fori_loop(0, 4, for_sibling, 0)
            part = pl.ds(4 * half, 4)
            got_yk.append(push(ysend.at[step, part], yk.at[step, part], [sibling]))
        for half in (0, 1):

            def for_own(j, _, half=half):
                ypart[4 * half + j] = target(distance(half, j), 0)
                return 0

            lax.fori_loop(0, 4, for_own, 0)
            if half == 0 and beside is not None:
                beside()
            got_yk[half]()
            part = pl.ds(4 * half, 4)
            total = ypart[part] + yk[step, part]
            rsend[step, part] = total.astype(BF16)
            if half:
                own = total[3]
            if step == 0:
                send_sums(step, half)
        if step:
            between()
            send_sums(step, 0)
            send_sums(step, 1)
        rbuf[step, z] = jnp.zeros((M, B), BF16)

        def result():
            for wait in got_r[step]:
                wait()
            return own + jnp.sum(rbuf[step].astype(F32), axis=0)

        return result

    summed = apply(0, got_u)()
    high = summed.astype(BF16)
    low = (summed - high.astype(F32)).astype(BF16)
    twice = nn(jnp.concatenate([high, low], axis=0), corr_gram_high, None)
    image_u = first_term_u + (twice[:M] + twice[M:] + nn(high, corr_gram_low, None))
    got_u = gather(1, image_u)
    uz[z] = ubuf[1, me_xy]
    got_uz = push(uz.at[z], uz.at[z], z_far, uz.at[pl.ds(0, NZ - 1)])
    image = first_term + by_halves(nn, summed, corr)
    ak[0] = nt(image, jnp.concatenate([basis, image], axis=0))
    got_ak = push(ak.at[0], ak.at[1], [sibling])
    energy_product = packed_product(image, energy * image)
    got_ak()
    asend[...] = (ak[0] + ak[1]).reshape(NZ, 8, B)
    az[z] = asend[z]
    got_az = push(
        lambda d: asend.at[(z + d + 1) % NZ], az.at[z], z_ring, az.at[pl.ds(0, NZ - 1)]
    )

    got_axy = []

    def beside():
        got_az()
        axy[me_xy] = jnp.sum(az[...], axis=0)
        got_axy.append(
            push(axy.at[me_xy], axy.at[me_xy], plane_far, axy.at[pl.ds(0, NXY - 1)])
        )

    got_hk = []

    def between():
        got_uz()
        images = jnp.concatenate(
            [uz[(z + d) % NZ] for d in (2, 3, 4, 5, 6, 7, 1, 0)], axis=1
        )
        sums = jnp.concatenate([rsend[1, i] for i in range(NZ)], axis=1)
        sums = jnp.concatenate([sums, sums], axis=0)
        hsend[...] = energy_product + packed_rows(nt(images, sums, None))
        got_hk.append(push(hsend, hk, [sibling]))

    second_sum = apply(1, got_u, beside, between)
    got_axy[0]()
    afull[z] = jnp.sum(axy[...], axis=0)
    got_afull = push(afull.at[z], afull.at[z], z_far, afull.at[pl.ds(0, NZ - 1)])
    got_hk[0]()
    hxy[me_xy] = hsend[...] + hk[...]
    got_hxy = push(hxy.at[me_xy], hxy.at[me_xy], plane_far, hxy.at[pl.ds(0, NXY - 1)])
    image_sum = energy * image + by_halves(nn, second_sum(), corr)
    got_hxy()
    hz[z] = jnp.sum(hxy[...], axis=0)
    got_hz = push(hz.at[z], hz.at[z], z_far, hz.at[pl.ds(0, NZ - 1)])
    got_afull()
    both = afull[...].reshape(M, B) * (1.0 / TOTAL)
    alpha_t = both[:, :M]
    square = pltpu.roll(both, M, axis=1)[:, :M]
    next_gram = square - nt(alpha_t, alpha_t)
    upper1, inverse1 = factor(jnp.concatenate([next_gram, next_gram], axis=1), fac.at[1])
    second = nn(inverse1, image - nn(alpha_t, basis))
    image_next = nn(inverse1, image_sum - nn(alpha_t, image)) - nn(upper1, basis)
    known = (
        nt(alpha_t, nn(alpha_t, alpha_t)) - nn(alpha_t, square) - nt(square, alpha_t)
    )
    coef_ref[0] = alpha_t
    coef_ref[1] = upper1
    across = lax.dot_general(
        inverse1, second, (((0,), (0,)), ((), ())), precision=HIGH, preferred_element_type=F32
    )
    got_hz()
    middle = unpacked(jnp.sum(hz[...], axis=0) * (1.0 / TOTAL))[:, :M] + known
    left = nn(inverse1, middle)
    residual_ref[...] = image_next - nn(left, across)
    coef_ref[2] = nt(left, inverse1)

    for i, like in sent:
        pltpu.make_async_copy(like, like, send.at[i]).wait()


def hand_over(residual_ref, coef_ref, residual_out, coef_out):
    residual_out[...] = residual_ref[...]
    for i in range(3):
        coef_out[i] = coef_ref[i].T


def on_device(coarse_kernel, correlations, neighbor, pair_weight, energies, start_block):
    vmem = pl.BlockSpec(memory_space=pltpu.VMEM)
    smem = pl.BlockSpec(memory_space=pltpu.SMEM)
    hbm = pl.BlockSpec(memory_space=pltpu.HBM)
    residual_t, coefficients_t = pl.pallas_call(
        kernel,
        out_shape=(
            jax.ShapeDtypeStruct((M, B), F32),
            jax.ShapeDtypeStruct((3, M, M), F32),
        ),
        in_specs=[hbm, hbm, smem, hbm, hbm, hbm],
        out_specs=(vmem, vmem),
        scratch_shapes=[
            pltpu.VMEM((M, M), BF16),
            pltpu.VMEM((1, B, B), BF16),
            pltpu.VMEM((16, 256), F32),
            pltpu.VMEM((1, B), F32),
            pltpu.VMEM((M, B), F32),
            pltpu.VMEM((8, 2, 4, 2, 2, 32, B), BF16),
            pltpu.VMEM((32, M), BF16),
            pltpu.VMEM((8, B), jnp.int32),
            pltpu.VMEM((8, B), jnp.int32),
            pltpu.VMEM((NXY, 8, B), jnp.int32),
            pltpu.VMEM((NZ, 8, B), jnp.int32),
            pltpu.SMEM((NXY, 8, B), jnp.int32),
            pltpu.SMEM((NZ, 8, B), jnp.int32),
            pltpu.VMEM((16, 256), F32),
            pltpu.SMEM((2, 16, 256), F32),
            pltpu.VMEM((2, M // 2, B), F32),
            pltpu.VMEM((NXY, M // 2, B), F32),
            pltpu.VMEM((NZ, M // 2, B), F32),
            pltpu.VMEM((M // 2, B), F32),
            pltpu.VMEM((2, M, B), F32),
            pltpu.VMEM((2, NXY, M, B), BF16),
            pltpu.VMEM((NXY, 8, M, B), F32),
            pltpu.VMEM((NZ, M, B), F32),
            pltpu.VMEM((2, NZ, M, B), F32),
            pltpu.VMEM((2, NZ, M, B), F32),
            pltpu.VMEM((2, NZ, M, B), BF16),
            pltpu.VMEM((2, NZ, M, B), BF16),
            pltpu.VMEM((NZ, M, B), BF16),
            pltpu.VMEM((2, M, B), F32),
            pltpu.VMEM((NZ, 8, B), F32),
            pltpu.VMEM((NZ, 8, B), F32),
            pltpu.VMEM((NXY, 8, B), F32),
            pltpu.VMEM((NZ, 8, B), F32),
            pltpu.VMEM((M // 2, B), F32),
            pltpu.VMEM((NXY, M // 2, B), F32),
            pltpu.VMEM((NZ, M // 2, B), F32),
            pltpu.VMEM((M // 2, B), F32),
            pltpu.SemaphoreType.DMA((64,)),
            pltpu.SemaphoreType.DMA((64,)),
            pltpu.SemaphoreType.DMA((9,)),
        ],
        compiler_params=pltpu.CompilerParams(
            collective_id=0, has_side_effects=True, vmem_limit_bytes=60 << 20
        ),
    )(coarse_kernel, correlations, neighbor, pair_weight, energies.reshape(1, B), start_block.T)
    residual_t, coefficients = pl.pallas_call(
        hand_over,
        out_shape=(
            jax.ShapeDtypeStruct((M, B), F32),
            jax.ShapeDtypeStruct((3, M, M), F32),
        ),
        in_specs=[vmem, vmem],
        out_specs=(vmem, vmem),
    )(residual_t, coefficients_t)
    return residual_t.T, coefficients


def solution(mesh):
    both = ("row", "col")
    return jax.shard_map(
        on_device,
        mesh=mesh,
        in_specs=(
            P("row", "col"),
            P(both, None, None),
            P(both),
            P("row", None),
            P(both),
            P(both, None),
        ),
        out_specs=(P(both, None), P()),
        check_vma=False,
    )
```

```python
import functools

import jax
import jax.numpy as jnp
from jax import lax
from jax.experimental import pallas as pl
from jax.experimental.pallas import tpu as pltpu
from jax.sharding import PartitionSpec as P

MESH = pl.DeviceIdType.MESH
HIGH = lax.Precision.HIGHEST
F32 = jnp.float32
BF16 = jnp.bfloat16
B = 128
M = 64
NX, NY, NZ = 4, 4, 8
NXY = NX * NY
TOTAL = 32768.0


def nn(a, b, precision=HIGH):
    return lax.dot_general(
        a, b, (((1,), (0,)), ((), ())), precision=precision, preferred_element_type=F32
    )


def nt(a, b, precision=HIGH):
    return lax.dot_general(
        a, b, (((1,), (1,)), ((), ())), precision=precision, preferred_element_type=F32
    )


def lanes(shape):
    return lax.broadcasted_iota(jnp.int32, shape, 1)


def rows(shape):
    return lax.broadcasted_iota(jnp.int32, shape, 0)


def by_halves(product, a, b):
    high = a.astype(BF16)
    low = (a - high.astype(F32)).astype(BF16)
    both = product(jnp.concatenate([high, low], axis=0), b, None)
    return both[: a.shape[0]] + both[a.shape[0] :]


def packed_product(left, right):
    return packed_rows(nt(left, jnp.concatenate([right, right], axis=0)))


def packed_rows(twice):
    upper, lower = twice[: M // 2], twice[M // 2 :]
    return jnp.where(lanes(upper.shape) < M, upper, lower)


def unpacked(packed):
    return jnp.concatenate([packed, pltpu.roll(packed, M, axis=1)], axis=0)


def factor(gram, out_ref):
    shape = (M, 2 * M)
    start = jnp.where(
        lanes(shape) < M, gram, jnp.where(lanes(shape) - M == rows(shape), 1.0, 0.0)
    )

    def four(matrix, s):
        c = [jnp.broadcast_to(matrix[:, s + i : s + i + 1], shape) for i in range(4)]
        r = [matrix[s + i : s + i + 1, :] for i in range(4)]
        p = [[c[j][s + i : s + i + 1, :] for j in range(4)] for i in range(4)]

        def pair(i):
            first, cross, last = p[i][i], p[i][i + 1], p[i + 1][i + 1]
            det = first * last - cross * cross
            root = lax.rsqrt(det)
            inverse = root * root
            scale = lax.rsqrt(first)
            upper = r[i] * scale
            lower = (r[i + 1] - r[i] * (cross * scale * scale)) * (root * first * scale)
            return last * inverse, -cross * inverse, first * inverse, [upper, lower]

        i00, i01, i11, done = pair(0)
        for i in (2, 3):
            w0 = p[0][i] * i00 + p[1][i] * i01
            w1 = p[0][i] * i01 + p[1][i] * i11
            r[i] = r[i] - w0 * r[0] - w1 * r[1]
            c[i] = c[i] - w0 * c[0] - w1 * c[1]
            for j in range(i, 4):
                p[i][j] = p[i][j] - w0 * p[0][j] - w1 * p[1][j]
        j00, j01, j11, more = pair(2)
        matrix = matrix - (
            c[0] * (i00 * r[0] + i01 * r[1])
            + c[1] * (i01 * r[0] + i11 * r[1])
            + c[2] * (j00 * r[2] + j01 * r[3])
            + c[3] * (j01 * r[2] + j11 * r[3])
        )
        return matrix, done + more

    def eight(block, matrix):
        matrix, done = four(matrix, 0)
        matrix, more = four(matrix, 4)
        finished = pltpu.roll(jnp.concatenate(done + more, axis=0), 8 * block, axis=1)
        out_ref[pl.ds(pl.multiple_of(8 * block, 8), 8), :] = finished
        matrix = jnp.concatenate([matrix[8:], matrix[:8]], axis=0)
        return pltpu.roll(matrix, 2 * M - 8, axis=1)

    lax.fori_loop(0, M // 8, eight, start)
    result = out_ref[...]
    upper = jnp.where(lanes(shape) >= rows(shape), result, 0.0)[:, :M]
    inverse = pltpu.roll(result, M, axis=1)[:, :M]
    return upper, inverse


def kernel(
    coarse_in, corr_in, near_ref, weight_in, energy_in, start_in,
    residual_ref, coef_ref,
    coarse_ref, corr_ref, weight_ref, energy_ref, start_ref,
    cbuf, chalf, near_k, near_own, near_xy, near_z, near_xy_s, near_z_s, w_other, w_s,
    gk, gxy, gz, gsend, fac,
    ubuf, tbuf, ypart, ysend, yk, rsend, rbuf,
    uz, ak, asend, az, axy, afull, hk, hxy, hz, hsend,
    send, recv, local,
):
    row, col = lax.axis_index("row"), lax.axis_index("col")
    z, yh = row // 2, row % 2
    yl, x, k = col // 8, (col // 2) % 4, col % 2
    y = yh * 2 + yl
    me_xy = y * NX + x

    def device(x_, y_, z_, k_):
        return (z_ * 2 + y_ // 2, (y_ % 2) * 8 + x_ * 2 + k_)

    sibling = device(x, y, z, 1 - k)
    x_ring = [device((x + d) % NX, y, z, k) for d in range(1, NX)]
    y_ring = [device(x, (y + d) % NY, z, k) for d in range(1, NY)]
    z_ring = [device(x, y, (z + d) % NZ, k) for d in range(1, NZ)]
    plane = [
        device((x + dx) % NX, (y + dy) % NY, z, k)
        for dy in range(NY)
        for dx in range(NX)
        if dx or dy
    ]
    away = sorted(
        (min(dx, NX - dx) + min(dy, NY - dy), dx, dy) for dy in range(NY) for dx in range(NX)
    )
    near_to_far = [
        [(dx, dy) for hops, dx, dy in away if low <= hops <= high]
        for low, high in ((0, 0), (1, 1), (2, 2), (3, 4))
    ]
    plane_far = [
        device((x + dx) % NX, (y + dy) % NY, z, k) for hops, dx, dy in away[::-1] if hops
    ]
    z_far = [z_ring[d - 1] for d in (4, 3, 5, 2, 6, 1, 7)]
    count = [0]
    sent = []
    pending = []

    def push(src, dst, targets, like=None):
        i = count[0]
        count[0] += 1
        for d, target in enumerate(targets):
            pltpu.make_async_remote_copy(
                src_ref=src(d) if callable(src) else src, dst_ref=dst,
                send_sem=send.at[i], recv_sem=recv.at[i],
                device_id=target, device_id_type=MESH,
            ).start()
        like = dst if like is None else like
        sent.append((i, like))

        def wait():
            pltpu.make_async_copy(like, like, recv.at[i]).wait()
            pending.remove(wait)

        pending.append(wait)
        return wait

    loads = [
        pltpu.make_async_copy(source, place, local.at[4 + i])
        for i, (source, place) in enumerate((
            (start_in, start_ref), (coarse_in, coarse_ref), (corr_in, corr_ref),
            (weight_in, weight_ref), (energy_in, energy_ref),
        ))
    ]
    for load in loads:
        load.start()
    barrier = pltpu.get_barrier_semaphore()
    partners = [sibling] + plane + z_ring
    for target in partners:
        pl.semaphore_signal(barrier, inc=1, device_id=target, device_id_type=MESH)
    near_own[...] = jnp.full((8, B), near_ref[0], jnp.int32)
    loads[0].wait()
    start_t = start_ref[...]
    gk[0] = packed_product(start_t, start_t)
    for load in loads[1:]:
        load.wait()
    pl.semaphore_wait(barrier, len(partners))

    other_half = pl.ds(pl.multiple_of((1 - k) * 32, 32), 32)
    own_half = pl.ds(pl.multiple_of(k * 32, 32), 32)
    got_gk = push(gk.at[0], gk.at[1], [sibling])
    got_half = push(coarse_ref.at[other_half], chalf, [sibling])
    got_near_k = push(near_own, near_k, [sibling])
    corr = corr_ref[0]
    start_u = by_halves(nt, start_t, corr)

    got_gk()
    gxy[me_xy] = gk[0] + gk[1]
    got_gxy = push(gxy.at[me_xy], gxy.at[me_xy], plane_far, gxy.at[pl.ds(0, NXY - 1)])

    got_half()
    shape = (M, B)
    place_own = jnp.where(lanes(shape) == rows(shape) + M * k, 1.0, 0.0).astype(BF16)
    place_sib = jnp.where(lanes(shape) == rows(shape) + M * (1 - k), 1.0, 0.0).astype(BF16)
    strip = nn(coarse_ref[own_half, :], place_own, None) + nn(chalf[...], place_sib, None)
    cbuf[z, yl, x, yh, k] = strip.astype(BF16)
    mine = cbuf.at[z, yl, x, yh, k]
    got_a = push(mine, mine, z_far, cbuf.at[pl.ds(0, 7), 0, 0, 0, 0])

    got_w = push(weight_ref, w_other, [y_ring[1]])
    near_xy[me_xy] = near_own[...]
    got_near_xy = push(near_xy.at[me_xy], near_xy.at[me_xy], plane_far, near_xy.at[pl.ds(0, NXY - 1)])
    got_near_k()
    near_z[z] = jnp.where(rows((8, B)) == 0, near_own[...], near_k[...])
    got_near_z = push(near_z.at[z], near_z.at[z], z_far, near_z.at[pl.ds(0, NZ - 1)])

    got_a()
    b_first = cbuf.at[pl.ds(0, 4), yl, x, yh, k]
    b_second = cbuf.at[pl.ds(4, 4), yl, x, yh, k]
    twelve = cbuf.at[pl.ds(0, 6), :, 0, 0, 0]
    got_b1 = push(b_first, b_first, [x_ring[i] for i in (1, 0, 2)], twelve)
    got_b2 = push(b_second, b_second, [y_ring[i] for i in (1, 0, 2)], twelve)

    got_gxy()
    gz[z] = jnp.sum(gxy[...], axis=0)
    got_gz = push(gz.at[z], gz.at[z], z_far, gz.at[pl.ds(0, NZ - 1)])

    def first_part(y_):
        return cbuf.at[pl.ds(0, 4), y_ % 2, :, y_ // 2, k]

    def second_part(x_):
        return cbuf.at[pl.ds(4, 4), :, x_, :, k]

    got_c, got_d = [], []
    got_b1()
    for d in (2, 1, 3):
        wait = push(first_part(y), first_part(y), [y_ring[d - 1]])
        got_c.append((d, wait, first_part((y - d) % NY)))
    got_b2()
    for d in (2, 1, 3):
        wait = push(second_part(x), second_part(x), [x_ring[d - 1]])
        got_c.append((d, wait, second_part((x - d) % NX)))
    got_c = [(wait, part) for d, wait, part in sorted(got_c, key=lambda e: e[0] == 2)]
    for part in (first_part(y), second_part(x)):
        got_d.append(push(part, part, [sibling]))

    got_w()
    got_near_xy()
    got_near_z()
    locals_ = [
        pltpu.make_async_copy(weight_ref, w_s.at[yh], local.at[0]),
        pltpu.make_async_copy(w_other, w_s.at[1 - yh], local.at[1]),
        pltpu.make_async_copy(near_xy, near_xy_s, local.at[2]),
        pltpu.make_async_copy(near_z, near_z_s, local.at[3]),
    ]
    for c in locals_:
        c.start()
        pending.append(c.wait)


    got_gz()
    gram = unpacked(jnp.sum(gz[...], axis=0) * (1.0 / TOTAL))
    _, inverse0 = factor(gram, fac.at[0])

    def gather(step, images):
        ubuf[step, me_xy] = images.astype(BF16)
        mine_ = ubuf.at[step, me_xy]
        waits = [None] * 3
        for g in (2, 1, 0):
            targets = [device((x + dx) % NX, (y + dy) % NY, z, k) for dx, dy in near_to_far[g + 1]]
            waits[g] = push(mine_, mine_, targets, ubuf.at[step, pl.ds(0, len(targets))])
        return waits

    got_u = gather(0, nn(inverse0, start_u))
    for wait, part in got_c:
        wait()
        got_d.append(push(part, part, [sibling]))
    for c in locals_:
        c.wait()
        pending.remove(c.wait)
    energy = energy_ref[...]
    basis = nn(inverse0, start_t)
    first_term = energy * basis
    first_term_u = by_halves(nt, first_term, corr)
    corr_gram = nt(corr, corr, None)
    corr_gram_high = corr_gram.astype(BF16)
    corr_gram_low = (corr_gram - corr_gram_high.astype(F32)).astype(BF16)
    for wait in got_d:
        wait()

    def distance(half, j):
        return j + 2 if half == 0 else jnp.where(j < 2, j + 6, 3 - j)

    got_r = {0: [], 1: []}

    def send_sums(step, half):
        entries = {0: (2, 1, 3, 0), 1: (4, 5, 6)}[half]
        targets = {0: (4, 3, 5, 2), 1: (6, 7, 1)}[half]
        got_r[step].append(push(
            lambda i: rsend.at[step, entries[i]], rbuf.at[step, z],
            [z_ring[d - 1] for d in targets], rbuf.at[step, pl.ds(0, len(targets))],
        ))

    def apply(step, got_u, beside=None, between=None):
        def one_source(dx, dy):
            q = (y + dy) % NY * NX + (x + dx) % NX
            block = cbuf[near_xy_s[q, 0, 0]].reshape(8, B, B)
            vector = ubuf[step, q]
            for c in range(8):
                tbuf[q, c] = nn(vector, block[c], None)

        for g, group in enumerate(near_to_far):
            if g:
                got_u[g - 1]()
            for dx, dy in group:
                one_source(dx, dy)

        def target(d, other):
            z_ = (z + d) % NZ
            near = near_z_s[z_, other, 0]
            place = z_ * 32 + yh * 16 + yl * 8 + x * 2 + (1 - k if other else k)
            total = jnp.zeros((M, B), F32)
            for q in range(NXY):
                qy, qx = q // NX, q % NX
                w = w_s[qy // 2, (qy % 2) * 8 + qx * 2 + k, place]
                total = total + w * tbuf[q, near]
            return total

        got_yk = []
        for half in (0, 1):

            def for_sibling(j, _, half=half):
                ysend[step, 4 * half + j] = target(distance(half, j), 1)
                return 0

            lax.fori_loop(0, 4, for_sibling, 0)
            part = pl.ds(4 * half, 4)
            got_yk.append(push(ysend.at[step, part], yk.at[step, part], [sibling]))
        for half in (0, 1):

            def for_own(j, _, half=half):
                ypart[4 * half + j] = target(distance(half, j), 0)
                return 0

            lax.fori_loop(0, 4, for_own, 0)
            if half == 0 and beside is not None:
                beside()
            got_yk[half]()
            part = pl.ds(4 * half, 4)
            total = ypart[part] + yk[step, part]
            rsend[step, part] = total.astype(BF16)
            if half:
                own = total[3]
            if step == 0:
                send_sums(step, half)
        if step:
            between()
            send_sums(step, 0)
            send_sums(step, 1)
        rbuf[step, z] = jnp.zeros((M, B), BF16)

        def result():
            for wait in got_r[step]:
                wait()
            return own + jnp.sum(rbuf[step].astype(F32), axis=0)

        return result

    summed = apply(0, got_u)()
    high = summed.astype(BF16)
    low = (summed - high.astype(F32)).astype(BF16)
    twice = nn(jnp.concatenate([high, low], axis=0), corr_gram_high, None)
    image_u = first_term_u + (twice[:M] + twice[M:] + nn(high, corr_gram_low, None))
    got_u = gather(1, image_u)
    uz[z] = ubuf[1, me_xy]
    got_uz = push(uz.at[z], uz.at[z], z_far, uz.at[pl.ds(0, NZ - 1)])
    image = first_term + by_halves(nn, summed, corr)
    ak[0] = nt(image, jnp.concatenate([basis, image], axis=0))
    got_ak = push(ak.at[0], ak.at[1], [sibling])
    energy_product = packed_product(image, energy * image)
    got_ak()
    asend[...] = (ak[0] + ak[1]).reshape(NZ, 8, B)
    az[z] = asend[z]
    got_az = push(
        lambda d: asend.at[(z + d + 1) % NZ], az.at[z], z_ring, az.at[pl.ds(0, NZ - 1)]
    )

    got_axy = []

    def beside():
        got_az()
        axy[me_xy] = jnp.sum(az[...], axis=0)
        got_axy.append(
            push(axy.at[me_xy], axy.at[me_xy], plane_far, axy.at[pl.ds(0, NXY - 1)])
        )

    got_hk = []

    def between():
        got_uz()
        images = jnp.concatenate(
            [uz[(z + d) % NZ] for d in (2, 3, 4, 5, 6, 7, 1, 0)], axis=1
        )
        sums = jnp.concatenate([rsend[1, i] for i in range(NZ)], axis=1)
        sums = jnp.concatenate([sums, sums], axis=0)
        hsend[...] = energy_product + packed_rows(nt(images, sums, None))
        got_hk.append(push(hsend, hk, [sibling]))

    second_sum = apply(1, got_u, beside, between)
    got_axy[0]()
    afull[z] = jnp.sum(axy[...], axis=0)
    got_afull = push(afull.at[z], afull.at[z], z_far, afull.at[pl.ds(0, NZ - 1)])
    got_hk[0]()
    hxy[me_xy] = hsend[...] + hk[...]
    got_hxy = push(hxy.at[me_xy], hxy.at[me_xy], plane_far, hxy.at[pl.ds(0, NXY - 1)])
    image_sum = energy * image + by_halves(nn, second_sum(), corr)
    got_hxy()
    hz[z] = jnp.sum(hxy[...], axis=0)
    got_hz = push(hz.at[z], hz.at[z], z_far, hz.at[pl.ds(0, NZ - 1)])
    got_afull()
    both = afull[...].reshape(M, B) * (1.0 / TOTAL)
    alpha_t = both[:, :M]
    square = pltpu.roll(both, M, axis=1)[:, :M]
    next_gram = square - nt(alpha_t, alpha_t)
    upper1, inverse1 = factor(jnp.concatenate([next_gram, next_gram], axis=1), fac.at[1])
    second = nn(inverse1, image - nn(alpha_t, basis))
    image_next = nn(inverse1, image_sum - nn(alpha_t, image)) - nn(upper1, basis)
    known = (
        nt(alpha_t, nn(alpha_t, alpha_t)) - nn(alpha_t, square) - nt(square, alpha_t)
    )
    coef_ref[0] = alpha_t
    coef_ref[1] = upper1
    across = lax.dot_general(
        inverse1, second, (((0,), (0,)), ((), ())), precision=HIGH, preferred_element_type=F32
    )
    got_hz()
    middle = unpacked(jnp.sum(hz[...], axis=0) * (1.0 / TOTAL))[:, :M] + known
    left = nn(inverse1, middle)
    residual_ref[...] = image_next - nn(left, across)
    coef_ref[2] = nt(left, inverse1)

    for i, like in sent:
        pltpu.make_async_copy(like, like, send.at[i]).wait()


def hand_over(residual_ref, coef_ref, residual_out, coef_out):
    residual_out[...] = residual_ref[...]
    for i in range(3):
        coef_out[i] = coef_ref[i].T


def on_device(coarse_kernel, correlations, neighbor, pair_weight, energies, start_block):
    vmem = pl.BlockSpec(memory_space=pltpu.VMEM)
    smem = pl.BlockSpec(memory_space=pltpu.SMEM)
    hbm = pl.BlockSpec(memory_space=pltpu.HBM)
    residual_t, coefficients_t = pl.pallas_call(
        kernel,
        out_shape=(
            jax.ShapeDtypeStruct((M, B), F32),
            jax.ShapeDtypeStruct((3, M, M), F32),
        ),
        in_specs=[hbm, hbm, smem, hbm, hbm, hbm],
        out_specs=(vmem, vmem),
        scratch_shapes=[
            pltpu.VMEM((M, M), BF16),
            pltpu.VMEM((1, B, B), BF16),
            pltpu.VMEM((16, 256), F32),
            pltpu.VMEM((1, B), F32),
            pltpu.VMEM((M, B), F32),
            pltpu.VMEM((8, 2, 4, 2, 2, 32, B), BF16),
            pltpu.VMEM((32, M), BF16),
            pltpu.VMEM((8, B), jnp.int32),
            pltpu.VMEM((8, B), jnp.int32),
            pltpu.VMEM((NXY, 8, B), jnp.int32),
            pltpu.VMEM((NZ, 8, B), jnp.int32),
            pltpu.SMEM((NXY, 8, B), jnp.int32),
            pltpu.SMEM((NZ, 8, B), jnp.int32),
            pltpu.VMEM((16, 256), F32),
            pltpu.SMEM((2, 16, 256), F32),
            pltpu.VMEM((2, M // 2, B), F32),
            pltpu.VMEM((NXY, M // 2, B), F32),
            pltpu.VMEM((NZ, M // 2, B), F32),
            pltpu.VMEM((M // 2, B), F32),
            pltpu.VMEM((2, M, B), F32),
            pltpu.VMEM((2, NXY, M, B), BF16),
            pltpu.VMEM((NXY, 8, M, B), F32),
            pltpu.VMEM((NZ, M, B), F32),
            pltpu.VMEM((2, NZ, M, B), F32),
            pltpu.VMEM((2, NZ, M, B), F32),
            pltpu.VMEM((2, NZ, M, B), BF16),
            pltpu.VMEM((2, NZ, M, B), BF16),
            pltpu.VMEM((NZ, M, B), BF16),
            pltpu.VMEM((2, M, B), F32),
            pltpu.VMEM((NZ, 8, B), F32),
            pltpu.VMEM((NZ, 8, B), F32),
            pltpu.VMEM((NXY, 8, B), F32),
            pltpu.VMEM((NZ, 8, B), F32),
            pltpu.VMEM((M // 2, B), F32),
            pltpu.VMEM((NXY, M // 2, B), F32),
            pltpu.VMEM((NZ, M // 2, B), F32),
            pltpu.VMEM((M // 2, B), F32),
            pltpu.SemaphoreType.DMA((64,)),
            pltpu.SemaphoreType.DMA((64,)),
            pltpu.SemaphoreType.DMA((9,)),
        ],
        compiler_params=pltpu.CompilerParams(
            collective_id=0, has_side_effects=True, vmem_limit_bytes=60 << 20
        ),
    )(coarse_kernel, correlations, neighbor, pair_weight, energies.reshape(1, B), start_block.T)
    residual_t, coefficients = pl.pallas_call(
        hand_over,
        out_shape=(
            jax.ShapeDtypeStruct((M, B), F32),
            jax.ShapeDtypeStruct((3, M, M), F32),
        ),
        in_specs=[vmem, vmem],
        out_specs=(vmem, vmem),
    )(residual_t, coefficients_t)
    return residual_t.T, coefficients


def solution(mesh):
    both = ("row", "col")
    return jax.shard_map(
        on_device,
        mesh=mesh,
        in_specs=(
            P("row", "col"),
            P(both, None, None),
            P(both),
            P("row", None),
            P(both),
            P(both, None),
        ),
        out_specs=(P(both, None), P()),
        check_vma=False,
    )
```
